128 devices in a mesh: dp: 16 (over y_lo, x, core), tensor: 8 (over z, y_hi).
Axes of the slice: x: 4, y: 4 (y_hi: 2, y_lo: 2; y = y_hi * 2 + y_lo), z: 4, core: 2. Of those that a mesh axis runs over, the one named last changes fastest.
Arguments:
- attn: bfloat16 [16, 1024, 6144], P('dp', None, 'tensor'), may hold values from -1.796875 to 1.796875
- w_out: bfloat16 [8192, 6144], P('dp', 'tensor'), may hold values from -0.09375 to 0.09375
- counts: int32 [8], replicated, may hold values from 1 to 6, 32 in all
- grad_out: bfloat16 [16, 1024, 8192], P('dp', 'tensor'), may hold values from -1.796875 to 1.796875
Outputs:
- projected: bfloat16 [16, 1024, 8192], P('dp', 'tensor')
- grad_attn: bfloat16 [16, 1024, 6144], P('dp', None, 'tensor')
- grad_w: float32 [8192, 6144], P('dp', 'tensor')
The draws below stay inside these ranges and needn't reach their ends.
Inputs may be any that keep to these rules, and one draw needn't show every extreme that they name: counts[r] is the number of live head slots of tensor rank r, its first ones; they sum to 32, and the largest is 6.
All inputs are finite; a program needn't handle non-finite values.
Results may differ from the reference program's by a relative error of at most 0.02.
Values may be sent and summed in bfloat16 or wider, within the bound.
No kernel may reach another device: no remote copies, remote signals or barrier semaphores. Data moves between devices by JAX's collectives and lax.ppermute only.
A program may use at most 256 MiB of HBM per device.

```python
import math
import jax
import jax.numpy as jnp
import numpy as np
from jax import lax

D = 8192
HD = 128
H = 32
S = 1024
CAP = 6
CHANNELS = 6144
N_DP = 16
N_TENSOR = 8


def strengthened(entries, rng, source, target, parts, factor):
    def block_of(position):
        return (jnp.arange(entries.shape[position]) // (entries.shape[position] // parts)).reshape((-1,) + (1,) * (entries.ndim - 1 - position))

    first = jax.random.permutation(rng, parts)[block_of(target)]
    second = (block_of(target) + parts // 2) % parts
    return jnp.where((block_of(source) == first) | (block_of(source) == second), factor * entries, entries)


def steps_of(own_key, extent, split, low, high):
    level, own = 1.0, jax.random.fold_in(own_key, 6)
    for dim, shards_of in split:
        draws = jnp.exp(jax.random.uniform(jax.random.fold_in(own, dim), (shards_of,), jnp.float32, low / len(split), high / len(split)))
        level = level * jnp.repeat(draws, extent[dim] // shards_of).reshape([-1 if axis == dim else 1 for axis in range(len(extent))])
    return level


def length_profile(number_of, total, limit, lean):
    portions = [(1 << 20) // math.isqrt(grade ** lean) + 1 for grade in range(2, number_of + 1)]
    rest, holding = total - limit - (number_of - 1), [1] * (number_of - 1)
    while rest > 0:
        candidates = [i for i in range(number_of - 1) if holding[i] < limit]
        mass, budget = sum([portions[i] for i in candidates]), rest
        for i in candidates:
            extra = min(limit - holding[i], max(1, budget * portions[i] // mass), rest)
            holding[i] = holding[i] + extra
            rest = rest - extra
    return np.array([limit] + holding)


def uneven(rng, number_of, total, reach, slope):
    if number_of == 2:
        one = jax.random.randint(rng, (), max(1, total - reach), min(reach, total - 1) + 1)
        return jnp.stack([one, total - one])
    lengths = jnp.asarray(length_profile(number_of, total, reach, slope), jnp.int32)
    couples = (number_of - 1) // 2
    source_of, receiver = lengths[1:1 + 2 * couples:2], lengths[2:2 + 2 * couples:2]
    room = jnp.minimum(source_of - 1, reach - receiver)
    shifted = jax.random.randint(jax.random.fold_in(rng, 1), (couples,), 0, 1 << 20) % (room + 1)
    lengths = lengths.at[1:1 + 2 * couples:2].set(source_of - shifted).at[2:2 + 2 * couples:2].set(receiver + shifted)
    return lengths[jax.random.permutation(jax.random.fold_in(rng, 2), number_of)]


def noise(key, dims, spread, bound, shards=(), held_as=jnp.bfloat16):
    result = spread * jax.random.normal(key, dims, jnp.float32)
    if shards:
        result = result * steps_of(key, dims, shards, -0.22, 0.18)
    return jnp.clip(result, -bound, bound).astype(held_as)


def noise_with(key, shape, spread, limit, pieces, heavy, kind=jnp.bfloat16):
    result = spread * jax.random.normal(key, shape, jnp.float32)
    if pieces:
        result = result * steps_of(key, shape, pieces, -0.22, 0.18)
    return jnp.clip(strengthened(result, jax.random.fold_in(key, 3), *heavy), -limit, limit).astype(kind)


def setup_inputs(seed: int = 0) -> dict:
    keys = jax.random.split(jax.random.key(seed), 5)
    return {
        "attn": noise_with(keys[0], (N_DP, S, CHANNELS), 0.3, 1.796875, ((0, 16), (2, 8)), (2, 1, 8, 2.0)),
        "w_out": noise(keys[1], (D, CHANNELS), (H * HD) ** -0.5, 0.09375, ((0, 16), (1, 8))),
        "counts": uneven(keys[2], N_TENSOR, H, CAP, 2).astype(jnp.int32),
        "grad_out": noise_with(keys[3], (N_DP, S, D), 0.3, 1.796875, ((0, 16), (1, 8)), (0, 2, 16, 2.0)),
    }


def live_mask():
    channel = jnp.arange(CAP * N_TENSOR * HD, dtype=jnp.int32)
    slot = channel // HD
    return slot, slot // CAP, slot % CAP


def reference(attn, w_out, counts, grad_out):
    slot, owner, within = live_mask()
    rank_count = jnp.take(counts, owner)
    live = (within < rank_count).astype(jnp.float32)
    masked = attn * live.astype(jnp.bfloat16)
    block = CAP * HD
    ranks = jnp.arange(N_TENSOR, dtype=jnp.int32)

    def per_group(total, group):
        rows = masked[group]
        cot = grad_out[group]

        def rank_term(carry, rank):
            part_a = lax.dynamic_slice_in_dim(rows, rank * block, block, 1)
            part_w = lax.dynamic_slice_in_dim(w_out, rank * block, block, 1)
            product = lax.dot_general(part_a, part_w, (((1,), (1,)), ((), ())), preferred_element_type=jnp.float32)
            product = lax.optimization_barrier(product.astype(jnp.bfloat16)).astype(jnp.float32)
            return carry + product, None

        summed, unused = lax.scan(rank_term, jnp.zeros((S, D), jnp.float32), ranks)
        projected = summed.astype(jnp.bfloat16)
        grad_rows = (jnp.dot(cot, w_out, preferred_element_type=jnp.float32) * live).astype(jnp.bfloat16)
        term = lax.dot_general(cot, rows, (((0,), (0,)), ((), ())), preferred_element_type=jnp.float32)
        term = lax.optimization_barrier(term.astype(jnp.bfloat16)).astype(jnp.float32)
        return total + term, (projected, grad_rows)

    groups = jnp.arange(N_DP, dtype=jnp.int32)
    grad_w, stacked = lax.scan(per_group, jnp.zeros((D, CAP * N_TENSOR * HD), jnp.float32), groups)
    return stacked[0], stacked[1], grad_w
```

```python
import jax
import jax.numpy as jnp
from jax import lax
from jax.sharding import PartitionSpec as P

HD = 128
NZ = 4
NH = 2


def ring(step):
    return [
        (z * NH + h, ((z + step) % NZ) * NH + h) for z in range(NZ) for h in range(NH)
    ]


SWAP = [(t, t ^ 1) for t in range(NZ * NH)]


def shift(value, step):
    return lax.ppermute(value, "tensor", ring(step))


def swap(value):
    return lax.ppermute(value, "tensor", SWAP)


def pick(blocks, index):
    return lax.dynamic_index_in_dim(blocks, index % NZ, 0, keepdims=False)


def per_device(attn, w_out, counts, grad_out):
    rank = lax.axis_index("tensor")
    z, h = rank // NH, rank % NH
    s, width = attn.shape[1:]
    own_rows, d = grad_out.shape[1:]
    n_dp = d // w_out.shape[0]
    piece = w_out.shape[0] // NZ
    feats = n_dp * piece
    half = s // 2

    own = jnp.sum(
        jnp.where(jnp.arange(counts.shape[0], dtype=jnp.int32) == rank, counts, 0)
    )
    live = (jnp.arange(width, dtype=jnp.int32) // HD < own).astype(jnp.float32)

    w_blocks = w_out.reshape(NZ, piece, width)
    w_near = [pick(w_blocks, z)] + [shift(pick(w_blocks, z + k), k) for k in range(1, NZ)]
    w_all = lax.all_gather(jnp.concatenate(w_near, axis=1), "dp", axis=0, tiled=True)

    g_blocks = grad_out[0].reshape(own_rows, n_dp, NZ, piece).transpose(2, 0, 1, 3)
    g_blocks = g_blocks.reshape(NZ, own_rows, feats)
    g_near = [pick(g_blocks, z)] + [shift(pick(g_blocks, z + k), k) for k in range(1, NZ)]
    g_far = [swap(block) for block in g_near]

    def in_order(pieces):
        stacked = jnp.stack(pieces)
        return [pick(stacked, z - a) for a in range(NZ)]

    cot = jnp.concatenate(in_order(g_far) + in_order(g_near), axis=0)

    rows = attn[0].reshape(NZ, NH, own_rows, width)
    other = lax.dynamic_index_in_dim(rows, 1 - h, 1, keepdims=False)
    same = lax.dynamic_index_in_dim(rows, h, 1, keepdims=False)
    masked = jnp.concatenate([other, same], axis=0).reshape(s, width) * live.astype(
        jnp.bfloat16
    )
    left = shift(masked, 1)
    right = shift(masked, -1)
    across = jnp.concatenate([shift(left[:half], 1), shift(right[half:], -1)], axis=0)
    act = jnp.concatenate([masked, left, across, right], axis=1)

    term = lax.dot_general(
        cot, act, (((0,), (0,)), ((), ())), preferred_element_type=jnp.float32
    ).astype(jnp.bfloat16)
    term = lax.psum_scatter(term, "dp", scatter_dimension=0, tiled=True)
    parts = [term[:, k * width : (k + 1) * width] for k in range(NZ)]
    parts = [parts[0]] + [shift(parts[k], -k) for k in range(1, NZ)]
    stacked = jnp.stack(parts)
    grad_w = jnp.concatenate([pick(stacked, a - z) for a in range(NZ)], axis=0).astype(
        jnp.float32
    )

    def rows_term(k):
        return jnp.dot(
            cot, w_all[:, k * width : (k + 1) * width], preferred_element_type=jnp.float32
        )

    far = rows_term(2).astype(jnp.bfloat16)
    up = shift(far[:half], 1)
    down = shift(far[half:], -1)
    to_right = rows_term(3)
    to_right = jnp.concatenate(
        [to_right[:half] + up.astype(jnp.float32), to_right[half:]], axis=0
    ).astype(jnp.bfloat16)
    to_left = rows_term(1)
    to_left = jnp.concatenate(
        [to_left[:half], to_left[half:] + down.astype(jnp.float32)], axis=0
    ).astype(jnp.bfloat16)
    total = (
        rows_term(0)
        + shift(to_right, 1).astype(jnp.float32)
        + shift(to_left, -1).astype(jnp.float32)
    )
    total = (total * live).astype(jnp.bfloat16).reshape(NH, NZ, own_rows, width)
    even = lax.dynamic_index_in_dim(total, 1 - h, 0, keepdims=False)
    odd = lax.dynamic_index_in_dim(total, h, 0, keepdims=False)
    grad_rows = jnp.stack([even, odd], axis=1).reshape(s, width)

    def project(x):
        return lax.dot_general(
            x, w_all, (((1,), (1,)), ((), ())), preferred_element_type=jnp.float32
        )

    sent = swap(project(act[:half]).astype(jnp.bfloat16))
    summed = (project(act[half:]) + sent.astype(jnp.float32)).astype(jnp.bfloat16)
    blocks = summed.reshape(NZ, own_rows, feats)
    quarters = [pick(blocks, z)] + [shift(pick(blocks, z + k), k) for k in range(1, NZ)]
    projected = jnp.stack(
        [q.reshape(own_rows, n_dp, piece) for q in in_order(quarters)], axis=2
    ).reshape(own_rows, d)
    return (projected[None], grad_rows[None], grad_w)


def solution(mesh):
    placed = (P("dp", None, "tensor"), P("dp", "tensor"), P(), P("dp", "tensor", None))
    return jax.shard_map(
        per_device,
        mesh=mesh,
        in_specs=placed,
        out_specs=(P("dp", "tensor", None), P("dp", None, "tensor"), P("dp", "tensor")),
        check_vma=False,
    )
```

```python
import jax
import jax.numpy as jnp
from jax import lax
from jax.sharding import PartitionSpec as P

HD = 128
NZ = 4
NH = 2


def ring(step):
    return [
        (z * NH + h, ((z + step) % NZ) * NH + h) for z in range(NZ) for h in range(NH)
    ]


SWAP = [(t, t ^ 1) for t in range(NZ * NH)]


def shift(value, step):
    return lax.ppermute(value, "tensor", ring(step))


def swap(value):
    return lax.ppermute(value, "tensor", SWAP)


def pick(blocks, index):
    return lax.dynamic_index_in_dim(blocks, index, 0, keepdims=False)


def f32_dot(a, b, dims):
    return lax.dot_general(a, b, (dims, ((), ())), preferred_element_type=jnp.float32)


def per_device(attn, w_out, counts, grad_out):
    rank = lax.axis_index("tensor")
    z, h = rank // NH, rank % NH
    s, width = attn.shape[1:]
    own_rows, d = grad_out.shape[1:]
    n_dp = d // w_out.shape[0]
    n_x = n_dp // 2
    piece = w_out.shape[0] // NZ
    feats = n_x * piece
    half = s // 2
    y = lax.axis_index("dp") // n_x
    groups = [list(range(n_x)), list(range(n_x, n_dp))]
    pair = [(i, (i + n_x) % n_dp) for i in range(n_dp)]

    own = jnp.sum(
        jnp.where(jnp.arange(counts.shape[0], dtype=jnp.int32) == rank, counts, 0)
    )
    live = (jnp.arange(width, dtype=jnp.int32) // HD < own).astype(jnp.float32)

    def in_order(pieces):
        stacked = jnp.stack(pieces)
        return [pick(stacked, (z - a) % NZ) for a in range(NZ)]

    w_blocks = w_out.reshape(NZ, piece, width)
    w_near = [pick(w_blocks, z)]
    w_near += [shift(pick(w_blocks, (z + k) % NZ), k) for k in range(1, NZ)]
    w_own = jnp.concatenate(w_near, axis=1)
    w_pair = lax.ppermute(w_own, "dp", pair)

    def gather(x):
        return lax.all_gather(x, "dp", axis=0, tiled=True, axis_index_groups=groups)

    w_all = [gather(w_own), gather(w_pair)]

    g = grad_out[0].reshape(own_rows, 2, n_x, NZ, piece)
    g = jnp.stack([lax.dynamic_index_in_dim(g, i, 1, keepdims=False) for i in (y, 1 - y)])
    g = g.transpose(3, 1, 0, 2, 4).reshape(NZ, own_rows, 2 * feats)
    g_near = [pick(g, z)] + [shift(pick(g, (z + k) % NZ), k) for k in range(1, NZ)]
    g_far = [swap(block) for block in g_near]
    cot = jnp.concatenate(in_order(g_far) + in_order(g_near), axis=0)
    cots = [cot[:, :feats], cot[:, feats:]]

    rows = attn[0].reshape(NZ, NH, own_rows, width)
    other = lax.dynamic_index_in_dim(rows, 1 - h, 1, keepdims=False)
    same = lax.dynamic_index_in_dim(rows, h, 1, keepdims=False)
    masked = jnp.concatenate([other, same], axis=0).reshape(s, width) * live.astype(
        jnp.bfloat16
    )
    left = shift(masked, 1)
    right = shift(masked, -1)
    across = jnp.concatenate([shift(left[:half], 1), shift(right[half:], -1)], axis=0)
    act = jnp.concatenate([masked, left, across, right], axis=1)

    def scatter(x):
        return lax.psum_scatter(
            x, "dp", scatter_dimension=0, tiled=True, axis_index_groups=groups
        )

    term_pair = scatter(f32_dot(cots[1], act, ((0,), (0,))).astype(jnp.bfloat16))
    term_pair = lax.ppermute(term_pair, "dp", pair)
    term_own = scatter(f32_dot(cots[0], act, ((0,), (0,))).astype(jnp.bfloat16))
    term = (term_own.astype(jnp.float32) + term_pair.astype(jnp.float32)).astype(
        jnp.bfloat16
    )
    parts = [term[:, k * width : (k + 1) * width] for k in range(NZ)]
    parts = [parts[0]] + [shift(parts[k], -k) for k in range(1, NZ)]
    stacked = jnp.stack(parts)
    grad_w = jnp.concatenate(
        [pick(stacked, (a - z) % NZ) for a in range(NZ)], axis=0
    ).astype(jnp.float32)

    def rows_term(k):
        cols = slice(k * width, (k + 1) * width)
        return sum(f32_dot(cots[i], w_all[i][:, cols], ((1,), (0,))) for i in range(2))

    far = rows_term(2).astype(jnp.bfloat16)
    up = shift(far[:half], 1)
    down = shift(far[half:], -1)
    to_right, to_left, stay = lax.optimization_barrier(
        (rows_term(3), rows_term(1), rows_term(0))
    )
    to_right = jnp.concatenate(
        [to_right[:half] + up.astype(jnp.float32), to_right[half:]], axis=0
    ).astype(jnp.bfloat16)
    to_left = jnp.concatenate(
        [to_left[:half], to_left[half:] + down.astype(jnp.float32)], axis=0
    ).astype(jnp.bfloat16)
    total = (
        stay
        + shift(to_right, 1).astype(jnp.float32)
        + shift(to_left, -1).astype(jnp.float32)
    )
    total = (total * live).astype(jnp.bfloat16).reshape(NH, NZ, own_rows, width)
    even = lax.dynamic_index_in_dim(total, 1 - h, 0, keepdims=False)
    odd = lax.dynamic_index_in_dim(total, h, 0, keepdims=False)
    grad_rows = jnp.stack([even, odd], axis=1).reshape(s, width)

    outs = []
    for i in range(2):
        sent = swap(f32_dot(act[:half], w_all[i], ((1,), (1,))).astype(jnp.bfloat16))
        kept = lax.optimization_barrier(f32_dot(act[half:], w_all[i], ((1,), (1,))))
        summed = (kept + sent.astype(jnp.float32)).astype(jnp.bfloat16)
        blocks = summed.reshape(NZ, own_rows, feats)
        quarters = [pick(blocks, z)]
        quarters += [shift(pick(blocks, (z + k) % NZ), k) for k in range(1, NZ)]
        quarters = [q.reshape(own_rows, n_x, piece) for q in in_order(quarters)]
        outs.append(jnp.stack(quarters, axis=2))
    outs = jnp.stack(outs)
    projected = jnp.stack([pick(outs, y), pick(outs, 1 - y)], axis=1)
    projected = projected.reshape(own_rows, d)
    return (projected[None], grad_rows[None], grad_w)


def solution(mesh):
    placed = (P("dp", None, "tensor"), P("dp", "tensor"), P(), P("dp", "tensor", None))
    return jax.shard_map(
        per_device,
        mesh=mesh,
        in_specs=placed,
        out_specs=(P("dp", "tensor", None), P("dp", None, "tensor"), P("dp", "tensor")),
        check_vma=False,
    )
```

```python
import jax
import jax.numpy as jnp
from jax import lax
from jax.experimental import pallas as pl
from jax.experimental.pallas import tpu as pltpu
from jax.sharding import PartitionSpec as P

HD = 128
NZ = 4
NH = 2
SWAP = [(t, t ^ 1) for t in range(NZ * NH)]
ANY = pl.BlockSpec(memory_space=pl.ANY)
SMEM = pl.BlockSpec(memory_space=pltpu.SMEM)
VMEM = pl.BlockSpec(memory_space=pltpu.VMEM)
LIMIT = 56 << 20


def ring(step):
    return [
        (z * NH + h, ((z + step) % NZ) * NH + h) for z in range(NZ) for h in range(NH)
    ]


def shift(value, step):
    return lax.ppermute(value, "tensor", ring(step))


def swap(value):
    return lax.ppermute(value, "tensor", SWAP)


def dot(a, b, dims):
    return lax.dot_general(a, b, (dims, ((), ())), preferred_element_type=jnp.float32)


def of(shape, dtype=jnp.bfloat16):
    return jax.ShapeDtypeStruct(shape, dtype)


def run(body, out, args, specs, after=(), grid=(), out_specs=VMEM, name=None, scratch=()):
    n, m = len(args), len(after)

    def kernel(*refs):
        body(*refs[:n], *refs[n + m :])

    return pl.pallas_call(
        kernel,
        out_shape=out,
        grid=grid,
        in_specs=list(specs) + [ANY] * m,
        out_specs=out_specs,
        scratch_shapes=list(scratch),
        name=name,
        cost_estimate=pl.CostEstimate(flops=1000, bytes_accessed=1000, transcendentals=0),
        compiler_params=pltpu.CompilerParams(vmem_limit_bytes=LIMIT),
    )(*args, *after)


def block(rows, start=0):
    return pl.ds(pl.multiple_of(start * rows, rows), rows)


def per_device(attn, w_out, counts, grad_out):
    rank = lax.axis_index("tensor")
    z, h = rank // NH, rank % NH
    s, width = attn.shape[1:]
    own_rows, d = grad_out.shape[1:]
    n_dp = d // w_out.shape[0]
    n_x = n_dp // 2
    piece = w_out.shape[0] // NZ
    feats = n_x * piece
    half = s // 2
    lanes = NZ * width
    y = lax.axis_index("dp") // n_x
    groups = [list(range(n_x)), list(range(n_x, n_dp))]
    pair = [(i, (i + n_x) % n_dp) for i in range(n_dp)]
    own = jnp.sum(
        jnp.where(jnp.arange(counts.shape[0], dtype=jnp.int32) == rank, counts, 0)
    )
    place = jnp.stack([z, h, y, own]).astype(jnp.int32)

    def split_w(place_ref, w_ref, *outs):
        for k in range(NZ):
            outs[k][...] = w_ref[block(piece, (place_ref[0] + k) % NZ), :]

    w_out4 = run(
        split_w, [of((piece, width))] * NZ, (place, w_out), [SMEM, VMEM],
        out_specs=[VMEM] * NZ, name="w_split",
    )
    w_near = [w_out4[0]] + [shift(w_out4[k], k) for k in range(1, NZ)]

    def split_g(place_ref, g_ref, *outs):
        for k in range(NZ):
            zk = (place_ref[0] + k) % NZ
            for i in range(2):
                first = ((place_ref[2] + i) % 2) * n_x
                for x in range(n_x):
                    outs[k][:, (i * n_x + x) * piece : (i * n_x + x + 1) * piece] = g_ref[
                        :, block(piece, (first + x) * NZ + zk)
                    ]

    g_out4 = run(
        split_g, [of((own_rows, 2 * feats))] * NZ, (place, grad_out[0]), [SMEM, VMEM],
        after=(w_out4[0],), out_specs=[VMEM] * NZ, name="g_split",
    )
    g_near = [g_out4[0]] + [shift(g_out4[k], k) for k in range(1, NZ)]

    def mask_body(place_ref, a_ref, *outs):
        slot = lax.broadcasted_iota(jnp.int32, (1, width), 1) // HD
        live = (slot < place_ref[3]).astype(jnp.float32).astype(jnp.bfloat16)
        for q in range(2):
            parity = (place_ref[1] + 1 + q) % NH
            for a in range(NZ):
                outs[q][a * own_rows : (a + 1) * own_rows, :] = (
                    a_ref[block(own_rows, a * NH + parity), :] * live
                )

    act = run(
        mask_body, [of((half, width))] * 2, (place, attn[0]), [SMEM, VMEM],
        after=(g_out4[0],), out_specs=[VMEM] * 2, name="mask",
    )
    left = [shift(act[0], 1), None]
    right = [None, shift(act[1], -1)]
    g_far = [swap(g) for g in g_near]

    def join_w(a, b, c, e, out_ref):
        for k, ref in enumerate((a, b, c, e)):
            out_ref[:, k * width : (k + 1) * width] = ref[...]

    w_own = run(
        join_w, of((piece, lanes)), w_near, [VMEM] * NZ, after=(act[0],), name="w_join"
    )

    def move(a_ref, out_ref):
        out_ref[...] = a_ref[...]

    w_pair = run(
        move, of((piece, lanes)), (lax.ppermute(w_own, "dp", pair),), [VMEM],
        after=(left[0], right[1], *g_near[1:], *g_far[:2]), name="w_move",
    )

    def gather(x):
        return lax.all_gather(x, "dp", axis=0, tiled=True, axis_index_groups=groups)

    w_all = [gather(w_own), gather(w_pair)]

    left[1] = shift(act[1], 1)
    right[0] = shift(act[0], -1)
    across = [shift(left[0], 1), shift(right[1], -1)]
    acts = [*act, *left, *across, *right]

    def join_g(place_ref, *refs):
        out_ref, sem = refs[2 * NZ], refs[2 * NZ + 1]
        copies = []
        for q in range(2):
            for k in range(NZ):
                row = q * NZ + (place_ref[0] + NZ - k) % NZ
                copies.append(
                    pltpu.make_async_copy(
                        refs[q * NZ + k], out_ref.at[block(own_rows, row), :], sem.at[q * NZ + k]
                    )
                )
        for copy in copies:
            copy.start()
        for copy in copies:
            copy.wait()

    cot = run(
        join_g, of((s, 2 * feats)), (place, *g_far, *g_near), [SMEM] + [ANY] * (2 * NZ),
        out_specs=ANY, name="g_join", scratch=[pltpu.SemaphoreType.DMA((2 * NZ,))],
    )

    tile = min(256, feats)
    steps = feats // tile

    def term_of(i, after):
        def body(g_ref, *refs):
            top, bottom, out_ref = g_ref[:half, :], g_ref[half:, :], refs[-1]
            for k in range(NZ):
                out_ref[:, k * width : (k + 1) * width] = (
                    dot(top, refs[2 * k][...], ((0,), (0,)))
                    + dot(bottom, refs[2 * k + 1][...], ((0,), (0,)))
                ).astype(jnp.bfloat16)

        return run(
            body, of((feats, lanes)), (cot, *acts),
            [pl.BlockSpec((s, tile), lambda j: (0, i * steps + j))] + [VMEM] * 8,
            after=after, grid=(steps,), out_specs=pl.BlockSpec((tile, lanes), lambda j: (j, 0)),
            name="term",
        )

    def project(i, after):
        def body(w_ref, *refs):
            for q in range(2):
                total = 0.0
                for k in range(NZ):
                    w = w_ref[:, k * width : (k + 1) * width]
                    total += dot(refs[2 * k + q][...], w, ((1,), (1,)))
                refs[8 + q][...] = total.astype(refs[8 + q].dtype)

        return run(
            body, [of((half, feats)), of((half, feats), jnp.float32)], (w_all[i], *acts),
            [pl.BlockSpec((tile, lanes), lambda j: (j, 0))] + [VMEM] * 8,
            after=after, grid=(steps,), out_specs=[pl.BlockSpec((half, tile), lambda j: (0, j))] * 2,
            name="project",
        )

    cols = width // 3 if width % 384 == 0 else width

    def rows_term(k, dtype, after, more=None, q=None):
        def body(g_ref, w_ref, v_ref, *refs):
            total = dot(g_ref[:, :feats], w_ref[...], ((1,), (0,)))
            total += dot(g_ref[:, feats:], v_ref[...], ((1,), (0,)))
            parts = [total[:half], total[half:]]
            if more is not None:
                parts[q] = parts[q] + refs[0][...].astype(jnp.float32)
            if len(outs) == 2:
                refs[-2][...] = parts[0].astype(dtype)
                refs[-1][...] = parts[1].astype(dtype)
            else:
                refs[-1][:half, :] = parts[0].astype(dtype)
                refs[-1][half:, :] = parts[1].astype(dtype)

        n = width // cols
        outs = [of((half, width), dtype)] * 2 if k else [of((s, width), dtype)]
        args = [cot, w_all[0], w_all[1]]
        column = pl.BlockSpec((feats, cols), lambda j: (0, k * n + j))
        specs = [VMEM, column, column]
        if more is not None:
            args.append(more)
            specs.append(pl.BlockSpec((half, cols), lambda j: (0, j)))
        got = run(
            body, outs, args, specs, after=after, grid=(n,),
            out_specs=[pl.BlockSpec((o.shape[0], cols), lambda j: (0, j)) for o in outs],
            name="rows_term",
        )
        return got if k else got[0]

    def scatter(x):
        return lax.psum_scatter(
            x, "dp", scatter_dimension=0, tiled=True, axis_index_groups=groups
        )

    term_pair = term_of(1, ())
    term_own = term_of(0, (term_pair,))
    far = rows_term(2, jnp.bfloat16, (term_own,))
    up = shift(far[0], 1)
    down = shift(far[1], -1)
    sent0, kept0 = project(0, (far[0],))
    got0 = swap(sent0)
    sent1, kept1 = project(1, (kept0,))
    got1 = swap(sent1)
    to_right = rows_term(3, jnp.bfloat16, (kept1,), up, 0)
    to_left = rows_term(1, jnp.bfloat16, (to_right[0],), down, 1)
    from_left = [shift(x, 1) for x in (to_right[1], to_right[0])][::-1]
    from_right = [shift(x, -1) for x in to_left]
    stay = rows_term(0, jnp.float32, (to_left[0],))
    term_pair = scatter(term_pair)
    term_own = scatter(term_own)

    def settle(place_ref, kept_ref, got_ref, *outs):
        for k in range(NZ):
            row = block(own_rows, (place_ref[0] + k) % NZ)
            outs[k][...] = (kept_ref[row, :] + got_ref[row, :].astype(jnp.float32)).astype(
                jnp.bfloat16
            )

    def spread(kept, got, after):
        outs = run(
            settle, [of((own_rows, feats))] * NZ, (place, kept, got), [SMEM, VMEM, VMEM],
            after=after, out_specs=[VMEM] * NZ, name="settle",
        )
        return [outs[0]] + [shift(outs[k], k) for k in range(1, NZ)], outs[0]

    quarters0, last = spread(kept0, got0, (stay, term_pair))
    term_pair = lax.ppermute(term_pair, "dp", pair)
    quarters1, last = spread(kept1, got1, (term_pair, last))

    def add_rows(place_ref, stay_ref, *refs):
        slot = lax.broadcasted_iota(jnp.int32, (1, width), 1) // HD
        live = (slot < place_ref[3]).astype(jnp.float32)
        for q in range(2):
            parity = (place_ref[1] + 1 + q) % NH
            for a in range(NZ):
                rows = slice(a * own_rows, (a + 1) * own_rows)
                total = (
                    stay_ref[q * half + a * own_rows : q * half + (a + 1) * own_rows, :]
                    + refs[q][rows, :].astype(jnp.float32)
                    + refs[2 + q][rows, :].astype(jnp.float32)
                )
                refs[4][block(own_rows, a * NH + parity), :] = (total * live).astype(
                    jnp.bfloat16
                )

    grad_rows = run(
        add_rows, of((s, width)), (place, stay, *from_left, *from_right), [SMEM] + [VMEM] * 5,
        after=(last,), name="add_rows",
    )

    def join_out(place_ref, *refs):
        out_ref = refs[-1]
        for i in range(2):
            first = ((place_ref[2] + i) % 2) * n_x
            for k in range(NZ):
                zk = (place_ref[0] + NZ - k) % NZ
                for x in range(n_x):
                    out_ref[:, block(piece, (first + x) * NZ + zk)] = refs[i * NZ + k][
                        :, x * piece : (x + 1) * piece
                    ]

    projected = run(
        join_out, of((own_rows, d)), (place, *quarters0, *quarters1),
        [SMEM] + [VMEM] * (2 * NZ), name="join_out",
    )

    def add_terms(a_ref, b_ref, *outs):
        for k in range(NZ):
            cols = slice(k * width, (k + 1) * width)
            outs[k][...] = (
                a_ref[:, cols].astype(jnp.float32) + b_ref[:, cols].astype(jnp.float32)
            ).astype(jnp.bfloat16)

    parts = run(
        add_terms, [of((piece, width))] * NZ, (term_own, term_pair), [VMEM] * 2,
        out_specs=[VMEM] * NZ, name="add_terms",
    )
    parts = [parts[0]] + [shift(parts[k], -k) for k in range(1, NZ)]

    def join_term(place_ref, *refs):
        for k in range(NZ):
            refs[-1][block(piece, (place_ref[0] + k) % NZ), :] = refs[k][...].astype(
                jnp.float32
            )

    grad_w = run(
        join_term, of((NZ * piece, width), jnp.float32), (place, *parts),
        [SMEM] + [VMEM] * NZ, name="join_term",
    )
    return (projected[None], grad_rows[None], grad_w)


def solution(mesh):
    placed = (P("dp", None, "tensor"), P("dp", "tensor"), P(), P("dp", "tensor", None))
    return jax.shard_map(
        per_device,
        mesh=mesh,
        in_specs=placed,
        out_specs=(P("dp", "tensor", None), P("dp", None, "tensor"), P("dp", "tensor")),
        check_vma=False,
    )
```

```python
import jax
import jax.numpy as jnp
from jax import lax
from jax.experimental import pallas as pl
from jax.experimental.pallas import tpu as pltpu
from jax.sharding import PartitionSpec as P

HD = 128
NZ = 4
NH = 2
SWAP = [(t, t ^ 1) for t in range(NZ * NH)]
ANY = pl.BlockSpec(memory_space=pl.ANY)
SMEM = pl.BlockSpec(memory_space=pltpu.SMEM)
VMEM = pl.BlockSpec(memory_space=pltpu.VMEM)
BIG = 48 << 20
SMALL = 32 << 20


def ring(step):
    return [
        (z * NH + h, ((z + step) % NZ) * NH + h) for z in range(NZ) for h in range(NH)
    ]


def shift(value, step):
    return lax.ppermute(value, "tensor", ring(step))


def swap(value):
    return lax.ppermute(value, "tensor", SWAP)


def dot(a, b, dims):
    return lax.dot_general(a, b, (dims, ((), ())), preferred_element_type=jnp.float32)


def of(shape, dtype=jnp.bfloat16):
    return jax.ShapeDtypeStruct(shape, dtype)


def run(body, out, args, specs, after=(), grid=(), out_specs=VMEM, name=None, limit=SMALL):
    n, m = len(args), len(after)

    def kernel(*refs):
        body(*refs[:n], *refs[n + m :])

    return pl.pallas_call(
        kernel,
        out_shape=out,
        grid=grid,
        in_specs=list(specs) + [ANY] * m,
        out_specs=out_specs,
        name=name,
        cost_estimate=pl.CostEstimate(flops=1000, bytes_accessed=1000, transcendentals=0),
        compiler_params=pltpu.CompilerParams(vmem_limit_bytes=limit),
    )(*args, *after)


def block(rows, start=0):
    return pl.ds(pl.multiple_of(start * rows, rows), rows)


def per_device(attn, w_out, counts, grad_out):
    rank = lax.axis_index("tensor")
    z, h = rank // NH, rank % NH
    s, width = attn.shape[1:]
    own_rows, d = grad_out.shape[1:]
    n_dp = d // w_out.shape[0]
    n_x = n_dp // 2
    piece = w_out.shape[0] // NZ
    feats = n_x * piece
    half = s // 2
    lanes = NZ * width
    y = lax.axis_index("dp") // n_x
    groups = [list(range(n_x)), list(range(n_x, n_dp))]
    pair = [(i, (i + n_x) % n_dp) for i in range(n_dp)]
    place = jnp.stack([z, h, y, rank]).astype(jnp.int32)

    def split_w(place_ref, w_ref, *outs):
        for k in range(NZ):
            outs[k][...] = w_ref[block(piece, (place_ref[0] + k) % NZ), :]

    w_out4 = run(
        split_w, [of((piece, width))] * NZ, (place, w_out), [SMEM, VMEM],
        out_specs=[VMEM] * NZ, name="w_split",
    )
    w_near = [w_out4[0]] + [shift(w_out4[k], k) for k in range(1, NZ)]

    def split_g(place_ref, g_ref, *outs):
        for k in range(NZ):
            zk = (place_ref[0] + k) % NZ
            for i in range(2):
                first = ((place_ref[2] + i) % 2) * n_x
                for x in range(n_x):
                    outs[k][:, (i * n_x + x) * piece : (i * n_x + x + 1) * piece] = g_ref[
                        :, block(piece, (first + x) * NZ + zk)
                    ]

    g_out4 = run(
        split_g, [of((own_rows, 2 * feats))] * NZ, (place, grad_out[0]), [SMEM, VMEM],
        after=(w_out4[0],), out_specs=[VMEM] * NZ, name="g_split",
    )
    g_near = [g_out4[0]] + [shift(g_out4[k], k) for k in range(1, NZ)]

    def mask_body(place_ref, counts_ref, a_ref, *outs):
        slot = lax.broadcasted_iota(jnp.int32, (1, width), 1) // HD
        live = (slot < counts_ref[place_ref[3]]).astype(jnp.float32).astype(jnp.bfloat16)
        for q in range(2):
            parity = (place_ref[1] + 1 + q) % NH
            for a in range(NZ):
                outs[q][a * own_rows : (a + 1) * own_rows, :] = (
                    a_ref[block(own_rows, a * NH + parity), :] * live
                )

    act = run(
        mask_body, [of((half, width))] * 2, (place, counts, attn[0]), [SMEM, SMEM, VMEM],
        after=(g_out4[0],), out_specs=[VMEM] * 2, name="mask",
    )
    left = [shift(act[0], 1), None]
    right = [None, shift(act[1], -1)]
    g_far = [swap(g) for g in g_near]

    def join_w(a, b, c, e, out_ref):
        for k, ref in enumerate((a, b, c, e)):
            out_ref[:, k * width : (k + 1) * width] = ref[...]

    w_own = run(
        join_w, of((piece, lanes)), w_near, [VMEM] * NZ, after=(act[0],), name="w_join"
    )

    def move(a_ref, out_ref):
        out_ref[...] = a_ref[...]

    w_pair = run(
        move, of((piece, lanes)), (lax.ppermute(w_own, "dp", pair),), [VMEM],
        after=(left[0], right[1], *g_near[1:], g_far[0]), name="w_move",
    )

    def gather(x):
        return lax.all_gather(x, "dp", axis=0, tiled=True, axis_index_groups=groups)

    w_all = [gather(w_own), gather(w_pair)]

    left[1] = shift(act[1], 1)
    right[0] = shift(act[0], -1)
    across = [shift(left[0], 1), shift(right[1], -1)]
    acts = [*act, *left, *across, *right]

    def join_g(place_ref, *refs):
        for q in range(2):
            for k in range(NZ):
                row = q * NZ + (place_ref[0] + NZ - k) % NZ
                refs[-1][block(own_rows, row), :] = refs[q * NZ + k][...]

    cot = run(
        join_g, of((s, 2 * feats)), (place, *g_far, *g_near), [SMEM] + [VMEM] * (2 * NZ),
        name="g_join",
    )

    tile = min(256, feats)
    steps = feats // tile

    def term_of(i, after):
        def body(g_ref, *refs):
            top, bottom, out_ref = g_ref[:half, :], g_ref[half:, :], refs[-1]
            for k in range(NZ):
                out_ref[:, k * width : (k + 1) * width] = (
                    dot(top, refs[2 * k][...], ((0,), (0,)))
                    + dot(bottom, refs[2 * k + 1][...], ((0,), (0,)))
                ).astype(jnp.bfloat16)

        return run(
            body, of((feats, lanes)), (cot, *acts),
            [pl.BlockSpec((s, tile), lambda j: (0, i * steps + j))] + [VMEM] * 8,
            after=after, grid=(steps,), out_specs=pl.BlockSpec((tile, lanes), lambda j: (j, 0)),
            name="term", limit=BIG,
        )

    def project(i, after):
        def body(w_ref, *refs):
            for q in range(2):
                total = 0.0
                for k in range(NZ):
                    w = w_ref[:, k * width : (k + 1) * width]
                    total += dot(refs[2 * k + q][...], w, ((1,), (1,)))
                refs[8 + q][...] = total.astype(refs[8 + q].dtype)

        return run(
            body, [of((half, feats)), of((half, feats), jnp.float32)], (w_all[i], *acts),
            [pl.BlockSpec((tile, lanes), lambda j: (j, 0))] + [VMEM] * 8,
            after=after, grid=(steps,), out_specs=[pl.BlockSpec((half, tile), lambda j: (0, j))] * 2,
            name="project", limit=BIG,
        )

    cols = width // 3 if width % 384 == 0 else width

    def rows_term(k, dtype, after, more=None, q=None):
        def body(g_ref, w_ref, v_ref, *refs):
            total = dot(g_ref[:, :feats], w_ref[...], ((1,), (0,)))
            total += dot(g_ref[:, feats:], v_ref[...], ((1,), (0,)))
            parts = [total[:half], total[half:]]
            if more is not None:
                parts[q] = parts[q] + refs[0][...].astype(jnp.float32)
            if len(outs) == 2:
                refs[-2][...] = parts[0].astype(dtype)
                refs[-1][...] = parts[1].astype(dtype)
            else:
                refs[-1][:half, :] = parts[0].astype(dtype)
                refs[-1][half:, :] = parts[1].astype(dtype)

        n = width // cols
        outs = [of((half, width), dtype)] * 2 if k else [of((s, width), dtype)]
        args = [cot, w_all[0], w_all[1]]
        column = pl.BlockSpec((feats, cols), lambda j: (0, k * n + j))
        specs = [VMEM, column, column]
        if more is not None:
            args.append(more)
            specs.append(pl.BlockSpec((half, cols), lambda j: (0, j)))
        got = run(
            body, outs, args, specs, after=after, grid=(n,),
            out_specs=[pl.BlockSpec((o.shape[0], cols), lambda j: (0, j)) for o in outs],
            name="rows_term", limit=BIG,
        )
        return got if k else got[0]

    def scatter(x):
        return lax.psum_scatter(
            x, "dp", scatter_dimension=0, tiled=True, axis_index_groups=groups
        )

    term_pair = term_of(1, ())
    term_own = term_of(0, (term_pair,))
    far = rows_term(2, jnp.bfloat16, (term_own,))
    up = shift(far[0], 1)
    down = shift(far[1], -1)
    sent0, kept0 = project(0, (far[0],))
    got0 = swap(sent0)
    stay = rows_term(0, jnp.float32, (kept0,))
    sent1, kept1 = project(1, (stay, up, down))
    got1 = swap(sent1)
    to_right = rows_term(3, jnp.bfloat16, (kept1,), up, 0)
    to_left = rows_term(1, jnp.bfloat16, (to_right[0],), down, 1)
    from_left = [shift(x, 1) for x in (to_right[1], to_right[0])][::-1]
    from_right = [shift(x, -1) for x in to_left]
    term_pair = scatter(term_pair)
    term_own = scatter(term_own)

    def settle(place_ref, kept_ref, got_ref, *outs):
        for k in range(NZ):
            row = block(own_rows, (place_ref[0] + k) % NZ)
            outs[k][...] = (kept_ref[row, :] + got_ref[row, :].astype(jnp.float32)).astype(
                jnp.bfloat16
            )

    def spread(kept, got, after):
        outs = run(
            settle, [of((own_rows, feats))] * NZ, (place, kept, got), [SMEM, VMEM, VMEM],
            after=after, out_specs=[VMEM] * NZ, name="settle",
        )
        return [outs[0]] + [shift(outs[k], k) for k in range(1, NZ)], outs[0]

    quarters0, last = spread(kept0, got0, (to_left[0], term_pair))
    term_pair = lax.ppermute(term_pair, "dp", pair)
    quarters1, last = spread(kept1, got1, (term_pair, last))

    def add_rows(place_ref, counts_ref, stay_ref, *refs):
        slot = lax.broadcasted_iota(jnp.int32, (1, width), 1) // HD
        live = (slot < counts_ref[place_ref[3]]).astype(jnp.float32)
        for q in range(2):
            parity = (place_ref[1] + 1 + q) % NH
            for a in range(NZ):
                rows = slice(a * own_rows, (a + 1) * own_rows)
                total = (
                    stay_ref[q * half + a * own_rows : q * half + (a + 1) * own_rows, :]
                    + refs[q][rows, :].astype(jnp.float32)
                    + refs[2 + q][rows, :].astype(jnp.float32)
                )
                refs[4][block(own_rows, a * NH + parity), :] = (total * live).astype(
                    jnp.bfloat16
                )

    grad_rows = run(
        add_rows, of((s, width)), (place, counts, stay, *from_left, *from_right), [SMEM] * 2 + [VMEM] * 5,
        after=(last,), name="add_rows",
    )

    def join_out(place_ref, *refs):
        out_ref = refs[-1]
        for i in range(2):
            first = ((place_ref[2] + i) % 2) * n_x
            for k in range(NZ):
                zk = (place_ref[0] + NZ - k) % NZ
                for x in range(n_x):
                    out_ref[:, block(piece, (first + x) * NZ + zk)] = refs[i * NZ + k][
                        :, x * piece : (x + 1) * piece
                    ]

    projected = run(
        join_out, of((own_rows, d)), (place, *quarters0, *quarters1),
        [SMEM] + [VMEM] * (2 * NZ), name="join_out",
    )

    def add_terms(a_ref, b_ref, *outs):
        for k in range(NZ):
            cols = slice(k * width, (k + 1) * width)
            outs[k][...] = (
                a_ref[:, cols].astype(jnp.float32) + b_ref[:, cols].astype(jnp.float32)
            ).astype(jnp.bfloat16)

    parts = run(
        add_terms, [of((piece, width))] * NZ, (term_own, term_pair), [VMEM] * 2,
        out_specs=[VMEM] * NZ, name="add_terms",
    )
    parts = [parts[0]] + [shift(parts[k], -k) for k in range(1, NZ)]

    def join_term(place_ref, *refs):
        for k in range(NZ):
            refs[-1][block(piece, (place_ref[0] + k) % NZ), :] = refs[k][...].astype(
                jnp.float32
            )

    grad_w = run(
        join_term, of((NZ * piece, width), jnp.float32), (place, *parts),
        [SMEM] + [VMEM] * NZ, name="join_term",
    )
    return (projected[None], grad_rows[None], grad_w)


def solution(mesh):
    placed = (P("dp", None, "tensor"), P("dp", "tensor"), P(), P("dp", "tensor", None))
    return jax.shard_map(
        per_device,
        mesh=mesh,
        in_specs=placed,
        out_specs=(P("dp", "tensor", None), P("dp", None, "tensor"), P("dp", "tensor")),
        check_vma=False,
    )
```

```python
import jax
import jax.numpy as jnp
from jax import lax
from jax.experimental import pallas as pl
from jax.experimental.pallas import tpu as pltpu
from jax.sharding import PartitionSpec as P

HD = 128
NZ = 4
NH = 2
SWAP = [(t, t ^ 1) for t in range(NZ * NH)]
ANY = pl.BlockSpec(memory_space=pl.ANY)
SMEM = pl.BlockSpec(memory_space=pltpu.SMEM)
VMEM = pl.BlockSpec(memory_space=pltpu.VMEM)
BIG = 56 << 20
SMALL = 56 << 20


def ring(step):
    return [
        (z * NH + h, ((z + step) % NZ) * NH + h) for z in range(NZ) for h in range(NH)
    ]


def shift(value, step):
    return lax.ppermute(value, "tensor", ring(step))


def swap(value):
    return lax.ppermute(value, "tensor", SWAP)


def dot(a, b, dims):
    return lax.dot_general(a, b, (dims, ((), ())), preferred_element_type=jnp.float32)


def of(shape, dtype=jnp.bfloat16):
    return jax.ShapeDtypeStruct(shape, dtype)


def run(body, out, args, specs, after=(), grid=(), out_specs=VMEM, name=None, limit=SMALL):
    n, m = len(args), len(after)

    def kernel(*refs):
        body(*refs[:n], *refs[n + m :])

    return pl.pallas_call(
        kernel,
        out_shape=out,
        grid=grid,
        in_specs=list(specs) + [ANY] * m,
        out_specs=out_specs,
        name=name,
        cost_estimate=pl.CostEstimate(flops=1000, bytes_accessed=1000, transcendentals=0),
        compiler_params=pltpu.CompilerParams(vmem_limit_bytes=limit),
    )(*args, *after)


def block(rows, start=0):
    return pl.ds(pl.multiple_of(start * rows, rows), rows)


def per_device(attn, w_out, counts, grad_out):
    rank = lax.axis_index("tensor")
    z, h = rank // NH, rank % NH
    s, width = attn.shape[1:]
    own_rows, d = grad_out.shape[1:]
    n_dp = d // w_out.shape[0]
    n_x = n_dp // 2
    piece = w_out.shape[0] // NZ
    feats = n_x * piece
    half = s // 2
    lanes = NZ * width
    y = lax.axis_index("dp") // n_x
    groups = [list(range(n_x)), list(range(n_x, n_dp))]
    pair = [(i, (i + n_x) % n_dp) for i in range(n_dp)]
    place = jnp.stack([z, h, y, rank]).astype(jnp.int32)

    def split_w(place_ref, w_ref, *outs):
        for k in range(NZ):
            outs[k][...] = w_ref[block(piece, (place_ref[0] + k) % NZ), :]

    w_out4 = run(
        split_w, [of((piece, width))] * NZ, (place, w_out), [SMEM, VMEM],
        out_specs=[VMEM] * NZ, name="w_split",
    )
    w_near = [w_out4[0]] + [shift(w_out4[k], k) for k in range(1, NZ)]

    def split_g(place_ref, g_ref, *outs):
        for k in range(NZ):
            zk = (place_ref[0] + k) % NZ
            for i in range(2):
                first = ((place_ref[2] + i) % 2) * n_x
                for x in range(n_x):
                    outs[k][:, (i * n_x + x) * piece : (i * n_x + x + 1) * piece] = g_ref[
                        :, block(piece, (first + x) * NZ + zk)
                    ]

    g_out4 = run(
        split_g, [of((own_rows, 2 * feats))] * NZ, (place, grad_out[0]), [SMEM, VMEM],
        after=(w_out4[0],), out_specs=[VMEM] * NZ, name="g_split",
    )
    g_near = [g_out4[0]] + [shift(g_out4[k], k) for k in range(1, NZ)]

    def mask_body(place_ref, counts_ref, a_ref, *outs):
        slot = lax.broadcasted_iota(jnp.int32, (1, width), 1) // HD
        live = (slot < counts_ref[place_ref[3]]).astype(jnp.float32).astype(jnp.bfloat16)
        for q in range(2):
            parity = (place_ref[1] + 1 + q) % NH
            for a in range(NZ):
                outs[q][a * own_rows : (a + 1) * own_rows, :] = (
                    a_ref[block(own_rows, a * NH + parity), :] * live
                )

    act = run(
        mask_body, [of((half, width))] * 2, (place, counts, attn[0]), [SMEM, SMEM, VMEM],
        after=(g_out4[0],), out_specs=[VMEM] * 2, name="mask",
    )
    left = [shift(act[0], 1), None]
    right = [None, shift(act[1], -1)]
    g_far = [swap(g) for g in g_near]

    def join_w(a, b, c, e, out_ref):
        for k, ref in enumerate((a, b, c, e)):
            out_ref[:, k * width : (k + 1) * width] = ref[...]

    w_own = run(
        join_w, of((piece, lanes)), w_near, [VMEM] * NZ, after=(act[0],), name="w_join"
    )

    def move(a_ref, out_ref):
        out_ref[...] = a_ref[...]

    w_pair = run(
        move, of((piece, lanes)), (lax.ppermute(w_own, "dp", pair),), [VMEM],
        after=(left[0], right[1], *g_near[1:], g_far[0]), name="w_move",
    )

    def gather(x):
        return lax.all_gather(x, "dp", axis=0, tiled=True, axis_index_groups=groups)

    w_all = [gather(w_own), gather(w_pair)]

    left[1] = shift(act[1], 1)
    right[0] = shift(act[0], -1)
    across = [shift(left[0], 1), shift(right[1], -1)]
    acts = [*act, *left, *across, *right]

    def join_g(place_ref, *refs):
        for q in range(2):
            for k in range(NZ):
                row = q * NZ + (place_ref[0] + NZ - k) % NZ
                refs[-1][block(own_rows, row), :] = refs[q * NZ + k][...]

    cot = run(
        join_g, of((s, 2 * feats)), (place, *g_far, *g_near), [SMEM] + [VMEM] * (2 * NZ),
        name="g_join",
    )

    tile = min(256, feats)
    steps = feats // tile

    def term_of(i, after):
        def body(g_ref, *refs):
            top, bottom, out_ref = g_ref[:half, :], g_ref[half:, :], refs[-1]
            for k in range(NZ):
                out_ref[:, k * width : (k + 1) * width] = (
                    dot(top, refs[2 * k][...], ((0,), (0,)))
                    + dot(bottom, refs[2 * k + 1][...], ((0,), (0,)))
                ).astype(jnp.bfloat16)

        return run(
            body, of((feats, lanes)), (cot, *acts),
            [pl.BlockSpec((s, tile), lambda j: (0, i * steps + j))] + [VMEM] * 8,
            after=after, grid=(steps,), out_specs=pl.BlockSpec((tile, lanes), lambda j: (j, 0)),
            name="term", limit=BIG,
        )

    def project(i, after):
        def body(w_ref, *refs):
            for q in range(2):
                total = 0.0
                for k in range(NZ):
                    w = w_ref[:, k * width : (k + 1) * width]
                    total += dot(refs[2 * k + q][...], w, ((1,), (1,)))
                refs[8 + q][...] = total.astype(refs[8 + q].dtype)

        return run(
            body, [of((half, feats)), of((half, feats), jnp.float32)], (w_all[i], *acts),
            [pl.BlockSpec((tile, lanes), lambda j: (j, 0))] + [VMEM] * 8,
            after=after, grid=(steps,), out_specs=[pl.BlockSpec((half, tile), lambda j: (0, j))] * 2,
            name="project", limit=BIG,
        )

    cols = width // 3 if width % 384 == 0 else width

    def rows_term(k, dtypes, after):
        def body(g_ref, w_ref, v_ref, *refs):
            total = dot(g_ref[:, :feats], w_ref[...], ((1,), (0,)))
            total += dot(g_ref[:, feats:], v_ref[...], ((1,), (0,)))
            if len(dtypes) == 2:
                refs[0][...] = total[:half].astype(dtypes[0])
                refs[1][...] = total[half:].astype(dtypes[1])
            else:
                refs[0][...] = total.astype(dtypes[0])

        n = width // cols
        outs = [of((s // len(dtypes), width), dtype) for dtype in dtypes]
        column = pl.BlockSpec((feats, cols), lambda j: (0, k * n + j))
        return run(
            body, outs, [cot, w_all[0], w_all[1]], [VMEM, column, column], after=after, grid=(n,),
            out_specs=[pl.BlockSpec((o.shape[0], cols), lambda j: (0, j)) for o in outs],
            name="rows_term", limit=BIG,
        )

    def scatter(x):
        return lax.psum_scatter(
            x, "dp", scatter_dimension=0, tiled=True, axis_index_groups=groups
        )

    term_pair = term_of(1, ())
    term_own = term_of(0, (term_pair,))
    sent0, kept0 = project(0, (term_own,))
    got0 = swap(sent0)
    bf16, f32 = jnp.bfloat16, jnp.float32
    far = rows_term(2, (bf16, bf16), (sent0,))
    up = shift(far[0], 1)
    down = shift(far[1], -1)
    right_top, right_bottom = rows_term(3, (f32, bf16), (far[0],))
    left_top, left_bottom = rows_term(1, (bf16, f32), (right_bottom,))
    from_left_bottom = shift(right_bottom, 1)
    from_right_top = shift(left_top, -1)

    def add_far(a_ref, up_ref, b_ref, down_ref, *outs):
        outs[0][...] = (a_ref[...] + up_ref[...].astype(jnp.float32)).astype(jnp.bfloat16)
        outs[1][...] = (b_ref[...] + down_ref[...].astype(jnp.float32)).astype(jnp.bfloat16)

    right_top, left_bottom = run(
        add_far, [of((half, width))] * 2, (right_top, up, left_bottom, down), [VMEM] * 4,
        after=(left_top,), out_specs=[VMEM] * 2, name="add_far",
    )
    from_left = [shift(right_top, 1), from_left_bottom]
    from_right = [from_right_top, shift(left_bottom, -1)]
    sent1, kept1 = project(1, (right_top,))
    got1 = swap(sent1)
    stay = rows_term(0, (f32,), (kept1,))[0]
    term_pair = scatter(term_pair)
    term_own = scatter(term_own)

    def settle(place_ref, kept_ref, got_ref, *outs):
        for k in range(NZ):
            row = block(own_rows, (place_ref[0] + k) % NZ)
            outs[k][...] = (kept_ref[row, :] + got_ref[row, :].astype(jnp.float32)).astype(
                jnp.bfloat16
            )

    def spread(kept, got, after):
        outs = run(
            settle, [of((own_rows, feats))] * NZ, (place, kept, got), [SMEM, VMEM, VMEM],
            after=after, out_specs=[VMEM] * NZ, name="settle",
        )
        return [outs[0]] + [shift(outs[k], k) for k in range(1, NZ)], outs[0]

    quarters0, last = spread(kept0, got0, (stay, term_pair, from_left_bottom, from_right_top))
    term_pair = lax.ppermute(term_pair, "dp", pair)
    quarters1, last = spread(kept1, got1, (term_pair, *quarters0[1:]))

    def add_rows(place_ref, counts_ref, stay_ref, *refs):
        slot = lax.broadcasted_iota(jnp.int32, (1, width), 1) // HD
        live = (slot < counts_ref[place_ref[3]]).astype(jnp.float32)
        for q in range(2):
            parity = (place_ref[1] + 1 + q) % NH
            for a in range(NZ):
                rows = slice(a * own_rows, (a + 1) * own_rows)
                total = (
                    stay_ref[q * half + a * own_rows : q * half + (a + 1) * own_rows, :]
                    + refs[q][rows, :].astype(jnp.float32)
                    + refs[2 + q][rows, :].astype(jnp.float32)
                )
                refs[4][block(own_rows, a * NH + parity), :] = (total * live).astype(
                    jnp.bfloat16
                )

    grad_rows = run(
        add_rows, of((s, width)), (place, counts, stay, *from_left, *from_right), [SMEM] * 2 + [VMEM] * 5,
        after=(last,), name="add_rows",
    )

    def join_out(place_ref, *refs):
        out_ref = refs[-1]
        for i in range(2):
            first = ((place_ref[2] + i) % 2) * n_x
            for k in range(NZ):
                zk = (place_ref[0] + NZ - k) % NZ
                for x in range(n_x):
                    out_ref[:, block(piece, (first + x) * NZ + zk)] = refs[i * NZ + k][
                        :, x * piece : (x + 1) * piece
                    ]

    projected = run(
        join_out, of((own_rows, d)), (place, *quarters0, *quarters1),
        [SMEM] + [VMEM] * (2 * NZ), name="join_out",
    )

    def add_terms(a_ref, b_ref, *outs):
        for k in range(NZ):
            cols = slice(k * width, (k + 1) * width)
            outs[k][...] = (
                a_ref[:, cols].astype(jnp.float32) + b_ref[:, cols].astype(jnp.float32)
            ).astype(jnp.bfloat16)

    parts = run(
        add_terms, [of((piece, width))] * NZ, (term_own, term_pair), [VMEM] * 2,
        after=(last,), out_specs=[VMEM] * NZ, name="add_terms",
    )
    parts = [parts[0]] + [shift(parts[k], -k) for k in range(1, NZ)]

    def join_term(place_ref, *refs):
        for k in range(NZ):
            refs[-1][block(piece, (place_ref[0] + k) % NZ), :] = refs[k][...].astype(
                jnp.float32
            )

    grad_w = run(
        join_term, of((NZ * piece, width), jnp.float32), (place, *parts),
        [SMEM] + [VMEM] * NZ, name="join_term",
    )
    return (projected[None], grad_rows[None], grad_w)


def solution(mesh):
    placed = (P("dp", None, "tensor"), P("dp", "tensor"), P(), P("dp", "tensor", None))
    return jax.shard_map(
        per_device,
        mesh=mesh,
        in_specs=placed,
        out_specs=(P("dp", "tensor", None), P("dp", None, "tensor"), P("dp", "tensor")),
        check_vma=False,
    )
```

```python
import jax
import jax.numpy as jnp
from jax import lax
from jax.experimental import pallas as pl
from jax.experimental.pallas import tpu as pltpu
from jax.sharding import PartitionSpec as P

HD = 128
NZ = 4
NH = 2
SWAP = [(t, t ^ 1) for t in range(NZ * NH)]
ANY = pl.BlockSpec(memory_space=pl.ANY)
SMEM = pl.BlockSpec(memory_space=pltpu.SMEM)
VMEM = pl.BlockSpec(memory_space=pltpu.VMEM)
BIG = 56 << 20
SMALL = 56 << 20


def ring(step):
    return [
        (z * NH + h, ((z + step) % NZ) * NH + h) for z in range(NZ) for h in range(NH)
    ]


def shift(value, step):
    return lax.ppermute(value, "tensor", ring(step))


def swap(value):
    return lax.ppermute(value, "tensor", SWAP)


def dot(a, b, dims):
    return lax.dot_general(a, b, (dims, ((), ())), preferred_element_type=jnp.float32)


def of(shape, dtype=jnp.bfloat16):
    return jax.ShapeDtypeStruct(shape, dtype)


def run(body, out, args, specs, after=(), grid=(), out_specs=VMEM, name=None, limit=SMALL):
    n, m = len(args), len(after)

    def kernel(*refs):
        body(*refs[:n], *refs[n + m :])

    return pl.pallas_call(
        kernel,
        out_shape=out,
        grid=grid,
        in_specs=list(specs) + [ANY] * m,
        out_specs=out_specs,
        name=name,
        cost_estimate=pl.CostEstimate(flops=1000, bytes_accessed=1000, transcendentals=0),
        compiler_params=pltpu.CompilerParams(vmem_limit_bytes=limit),
    )(*args, *after)


def block(rows, start=0):
    return pl.ds(pl.multiple_of(start * rows, rows), rows)


def per_device(attn, w_out, counts, grad_out):
    rank = lax.axis_index("tensor")
    z, h = rank // NH, rank % NH
    s, width = attn.shape[1:]
    own_rows, d = grad_out.shape[1:]
    n_dp = d // w_out.shape[0]
    n_x = n_dp // 2
    piece = w_out.shape[0] // NZ
    feats = n_x * piece
    half = s // 2
    lanes = NZ * width
    y = lax.axis_index("dp") // n_x
    groups = [list(range(n_x)), list(range(n_x, n_dp))]
    pair = [(i, (i + n_x) % n_dp) for i in range(n_dp)]
    place = jnp.stack([z, h, y, rank]).astype(jnp.int32)

    def split(place_ref, w_ref, g_ref, w0_ref, g0_ref, *outs):
        for k in range(NZ):
            zk = (place_ref[0] + k) % NZ
            w_to, g_to, at = (outs[k - 1], outs[k - 1], width) if k else (w0_ref, g0_ref, 0)
            w_to[:, :width] = w_ref[block(piece, zk), :]
            for i in range(2):
                first = ((place_ref[2] + i) % 2) * n_x
                for x in range(n_x):
                    col = at + (i * n_x + x) * piece
                    g_to[:, col : col + piece] = g_ref[:, block(piece, (first + x) * NZ + zk)]

    w_own, g_own, *packs = run(
        split,
        [of((piece, width)), of((piece, 2 * feats))] + [of((piece, width + 2 * feats))] * 3,
        (place, w_out, grad_out[0]), [SMEM, VMEM, VMEM], out_specs=[VMEM] * 5, name="split",
    )
    packs = [shift(packs[k - 1], k) for k in range(1, NZ)]

    def mask_body(place_ref, counts_ref, a_ref, *outs):
        slot = lax.broadcasted_iota(jnp.int32, (1, width), 1) // HD
        live = (slot < counts_ref[place_ref[3]]).astype(jnp.float32).astype(jnp.bfloat16)
        for q in range(2):
            parity = (place_ref[1] + 1 + q) % NH
            for a in range(NZ):
                outs[q][a * own_rows : (a + 1) * own_rows, :] = (
                    a_ref[block(own_rows, a * NH + parity), :] * live
                )

    act = run(
        mask_body, [of((half, width))] * 2, (place, counts, attn[0]), [SMEM, SMEM, VMEM],
        after=(w_own,), out_specs=[VMEM] * 2, name="mask",
    )
    left = [shift(act[0], 1), None]
    right = [None, shift(act[1], -1)]
    g_far = [swap(g_own)]

    def unpack(w0_ref, *refs):
        packed, outs = refs[: NZ - 1], refs[NZ - 1 :]
        outs[0][:, :width] = w0_ref[...]
        for k in range(1, NZ):
            outs[0][:, k * width : (k + 1) * width] = packed[k - 1][:, :width]
            outs[k][...] = packed[k - 1][:, width:]

    w_own, *g_near = run(
        unpack, [of((piece, lanes))] + [of((piece, 2 * feats))] * 3, (w_own, *packs),
        [VMEM] * NZ, after=(act[0], g_far[0]), out_specs=[VMEM] * NZ, name="unpack",
    )
    g_far += [swap(g) for g in g_near]
    g_near = [g_own, *g_near]

    def move(a_ref, out_ref):
        out_ref[...] = a_ref[...]

    w_pair = run(
        move, of((piece, lanes)), (lax.ppermute(w_own, "dp", pair),), [VMEM],
        after=(left[0], right[1], g_far[1], g_far[3]), name="w_move",
    )

    def gather(x):
        return lax.all_gather(x, "dp", axis=0, tiled=True, axis_index_groups=groups)

    w_all = [gather(w_own), gather(w_pair)]

    left[1] = shift(act[1], 1)
    right[0] = shift(act[0], -1)
    across = [shift(left[0], 1), shift(right[1], -1)]
    acts = [*act, *left, *across, *right]

    def join_g(place_ref, *refs):
        for q in range(2):
            for k in range(NZ):
                row = q * NZ + (place_ref[0] + NZ - k) % NZ
                refs[-1][block(own_rows, row), :] = refs[q * NZ + k][...]

    cot = run(
        join_g, of((s, 2 * feats)), (place, *g_far, *g_near), [SMEM] + [VMEM] * (2 * NZ),
        name="g_join",
    )

    tile = min(256, feats)
    steps = feats // tile

    def term_of(i, after):
        def body(g_ref, *refs):
            top, bottom, out_ref = g_ref[:half, :], g_ref[half:, :], refs[-1]
            for k in range(NZ):
                out_ref[:, k * width : (k + 1) * width] = (
                    dot(top, refs[2 * k][...], ((0,), (0,)))
                    + dot(bottom, refs[2 * k + 1][...], ((0,), (0,)))
                ).astype(jnp.bfloat16)

        return run(
            body, of((feats, lanes)), (cot, *acts),
            [pl.BlockSpec((s, tile), lambda j: (0, i * steps + j))] + [VMEM] * 8,
            after=after, grid=(steps,), out_specs=pl.BlockSpec((tile, lanes), lambda j: (j, 0)),
            name="term", limit=BIG,
        )

    def project(i, after):
        def body(w_ref, *refs):
            for q in range(2):
                total = 0.0
                for k in range(NZ):
                    w = w_ref[:, k * width : (k + 1) * width]
                    total += dot(refs[2 * k + q][...], w, ((1,), (1,)))
                refs[8 + q][...] = total.astype(refs[8 + q].dtype)

        return run(
            body, [of((half, feats)), of((half, feats), jnp.float32)], (w_all[i], *acts),
            [pl.BlockSpec((tile, lanes), lambda j: (j, 0))] + [VMEM] * 8,
            after=after, grid=(steps,), out_specs=[pl.BlockSpec((half, tile), lambda j: (0, j))] * 2,
            name="project", limit=BIG,
        )

    cols = width // 3 if width % 384 == 0 else width

    def rows_term(k, dtypes, after):
        def body(g_ref, w_ref, v_ref, *refs):
            total = dot(g_ref[:, :feats], w_ref[...], ((1,), (0,)))
            total += dot(g_ref[:, feats:], v_ref[...], ((1,), (0,)))
            if len(dtypes) == 2:
                refs[0][...] = total[:half].astype(dtypes[0])
                refs[1][...] = total[half:].astype(dtypes[1])
            else:
                refs[0][...] = total.astype(dtypes[0])

        n = width // cols
        outs = [of((s // len(dtypes), width), dtype) for dtype in dtypes]
        column = pl.BlockSpec((feats, cols), lambda j: (0, k * n + j))
        return run(
            body, outs, [cot, w_all[0], w_all[1]], [VMEM, column, column], after=after, grid=(n,),
            out_specs=[pl.BlockSpec((o.shape[0], cols), lambda j: (0, j)) for o in outs],
            name="rows_term", limit=BIG,
        )

    def scatter(x):
        return lax.psum_scatter(
            x, "dp", scatter_dimension=0, tiled=True, axis_index_groups=groups
        )

    def settle(place_ref, kept_ref, got_ref, *outs):
        for k in range(NZ):
            row = block(own_rows, (place_ref[0] + k) % NZ)
            outs[k][...] = (kept_ref[row, :] + got_ref[row, :].astype(jnp.float32)).astype(
                jnp.bfloat16
            )

    def spread(kept, got, after):
        outs = run(
            settle, [of((own_rows, feats))] * NZ, (place, kept, got), [SMEM, VMEM, VMEM],
            after=after, out_specs=[VMEM] * NZ, name="settle",
        )
        return [outs[0]] + [shift(outs[k], k) for k in range(1, NZ)], outs[0]

    sent0, kept0 = project(0, ())
    got0 = swap(sent0)
    term_pair = term_of(1, (sent0,))
    term_own = term_of(0, (term_pair,))
    quarters0, last = spread(kept0, got0, (term_own,))
    bf16, f32 = jnp.bfloat16, jnp.float32
    far = rows_term(2, (bf16, bf16), (last,))
    up = shift(far[0], 1)
    down = shift(far[1], -1)
    right_top, right_bottom = rows_term(3, (f32, bf16), (far[0],))
    left_top, left_bottom = rows_term(1, (bf16, f32), (right_bottom, *quarters0[1:]))
    from_left_bottom = shift(right_bottom, 1)
    from_right_top = shift(left_top, -1)

    def add_far(a_ref, up_ref, b_ref, down_ref, *outs):
        outs[0][...] = (a_ref[...] + up_ref[...].astype(jnp.float32)).astype(jnp.bfloat16)
        outs[1][...] = (b_ref[...] + down_ref[...].astype(jnp.float32)).astype(jnp.bfloat16)

    right_top, left_bottom = run(
        add_far, [of((half, width))] * 2, (right_top, up, left_bottom, down), [VMEM] * 4,
        after=(left_top,), out_specs=[VMEM] * 2, name="add_far",
    )
    from_left = [shift(right_top, 1), from_left_bottom]
    from_right = [from_right_top, shift(left_bottom, -1)]
    sent1, kept1 = project(1, (right_top,))
    got1 = swap(sent1)
    stay = rows_term(0, (f32,), (kept1,))[0]
    term_pair = scatter(term_pair)
    term_own = scatter(term_own)

    term_pair = lax.ppermute(term_pair, "dp", pair)
    quarters1, last = spread(kept1, got1, (stay, term_pair, from_left_bottom, from_right_top))

    def add_rows(place_ref, counts_ref, stay_ref, *refs):
        slot = lax.broadcasted_iota(jnp.int32, (1, width), 1) // HD
        live = (slot < counts_ref[place_ref[3]]).astype(jnp.float32)
        for q in range(2):
            parity = (place_ref[1] + 1 + q) % NH
            for a in range(NZ):
                rows = slice(a * own_rows, (a + 1) * own_rows)
                total = (
                    stay_ref[q * half + a * own_rows : q * half + (a + 1) * own_rows, :]
                    + refs[q][rows, :].astype(jnp.float32)
                    + refs[2 + q][rows, :].astype(jnp.float32)
                )
                refs[4][block(own_rows, a * NH + parity), :] = (total * live).astype(
                    jnp.bfloat16
                )

    grad_rows = run(
        add_rows, of((s, width)), (place, counts, stay, *from_left, *from_right), [SMEM] * 2 + [VMEM] * 5,
        after=(last,), name="add_rows",
    )

    def join_out(place_ref, *refs):
        out_ref = refs[-1]
        for i in range(2):
            first = ((place_ref[2] + i) % 2) * n_x
            for k in range(NZ):
                zk = (place_ref[0] + NZ - k) % NZ
                for x in range(n_x):
                    out_ref[:, block(piece, (first + x) * NZ + zk)] = refs[i * NZ + k][
                        :, x * piece : (x + 1) * piece
                    ]

    projected = run(
        join_out, of((own_rows, d)), (place, *quarters0, *quarters1),
        [SMEM] + [VMEM] * (2 * NZ), name="join_out",
    )

    def add_terms(a_ref, b_ref, *outs):
        for k in range(NZ):
            cols = slice(k * width, (k + 1) * width)
            outs[k][...] = (
                a_ref[:, cols].astype(jnp.float32) + b_ref[:, cols].astype(jnp.float32)
            ).astype(jnp.bfloat16)

    parts = run(
        add_terms, [of((piece, width))] * NZ, (term_own, term_pair), [VMEM] * 2,
        after=(last,), out_specs=[VMEM] * NZ, name="add_terms",
    )
    parts = [parts[0]] + [shift(parts[k], -k) for k in range(1, NZ)]

    def join_term(place_ref, *refs):
        for k in range(NZ):
            refs[-1][block(piece, (place_ref[0] + k) % NZ), :] = refs[k][...].astype(
                jnp.float32
            )

    grad_w = run(
        join_term, of((NZ * piece, width), jnp.float32), (place, *parts),
        [SMEM] + [VMEM] * NZ, name="join_term",
    )
    return (projected[None], grad_rows[None], grad_w)


def solution(mesh):
    placed = (P("dp", None, "tensor"), P("dp", "tensor"), P(), P("dp", "tensor", None))
    return jax.shard_map(
        per_device,
        mesh=mesh,
        in_specs=placed,
        out_specs=(P("dp", "tensor", None), P("dp", None, "tensor"), P("dp", "tensor")),
        check_vma=False,
    )
```

```python
import jax
import jax.numpy as jnp
from jax import lax
from jax.experimental import pallas as pl
from jax.experimental.pallas import tpu as pltpu
from jax.sharding import PartitionSpec as P

HD = 128
NZ = 4
NH = 2
SWAP = [(t, t ^ 1) for t in range(NZ * NH)]
ANY = pl.BlockSpec(memory_space=pl.ANY)
SMEM = pl.BlockSpec(memory_space=pltpu.SMEM)
VMEM = pl.BlockSpec(memory_space=pltpu.VMEM)
BIG = 56 << 20
SMALL = 56 << 20


def ring(step):
    return [
        (z * NH + h, ((z + step) % NZ) * NH + h) for z in range(NZ) for h in range(NH)
    ]


def shift(value, step):
    return lax.ppermute(value, "tensor", ring(step))


def swap(value):
    return lax.ppermute(value, "tensor", SWAP)


def dot(a, b, dims):
    return lax.dot_general(a, b, (dims, ((), ())), preferred_element_type=jnp.float32)


def of(shape, dtype=jnp.bfloat16):
    return jax.ShapeDtypeStruct(shape, dtype)


def run(body, out, args, specs, after=(), grid=(), out_specs=VMEM, name=None, limit=SMALL):
    n, m = len(args), len(after)

    def kernel(*refs):
        body(*refs[:n], *refs[n + m :])

    return pl.pallas_call(
        kernel,
        out_shape=out,
        grid=grid,
        in_specs=list(specs) + [ANY] * m,
        out_specs=out_specs,
        name=name,
        cost_estimate=pl.CostEstimate(flops=1000, bytes_accessed=1000, transcendentals=0),
        compiler_params=pltpu.CompilerParams(vmem_limit_bytes=limit),
    )(*args, *after)


def block(rows, start=0):
    return pl.ds(pl.multiple_of(start * rows, rows), rows)


def per_device(attn, w_out, counts, grad_out):
    rank = lax.axis_index("tensor")
    z, h = rank // NH, rank % NH
    s, width = attn.shape[1:]
    own_rows, d = grad_out.shape[1:]
    n_dp = d // w_out.shape[0]
    n_x = n_dp // 2
    piece = w_out.shape[0] // NZ
    feats = n_x * piece
    half = s // 2
    lanes = NZ * width
    y = lax.axis_index("dp") // n_x
    groups = [list(range(n_x)), list(range(n_x, n_dp))]
    pair = [(i, (i + n_x) % n_dp) for i in range(n_dp)]
    place = jnp.stack([z, h, y, rank]).astype(jnp.int32)

    def split_w(place_ref, w_ref, *outs):
        for k in range(NZ):
            outs[k][...] = w_ref[block(piece, (place_ref[0] + k) % NZ), :]

    w_out4 = run(
        split_w, [of((piece, width))] * NZ, (place, w_out), [SMEM, VMEM],
        out_specs=[VMEM] * NZ, name="w_split",
    )
    w_near = [w_out4[0]] + [shift(w_out4[k], k) for k in range(1, NZ)]

    def split_g(place_ref, g_ref, *outs):
        for k in range(NZ):
            zk = (place_ref[0] + k) % NZ
            for i in range(2):
                first = ((place_ref[2] + i) % 2) * n_x
                for x in range(n_x):
                    outs[k][:, (i * n_x + x) * piece : (i * n_x + x + 1) * piece] = g_ref[
                        :, block(piece, (first + x) * NZ + zk)
                    ]

    g_out4 = run(
        split_g, [of((own_rows, 2 * feats))] * NZ, (place, grad_out[0]), [SMEM, VMEM],
        after=(w_out4[0],), out_specs=[VMEM] * NZ, name="g_split",
    )
    g_near = [g_out4[0]] + [shift(g_out4[k], k) for k in range(1, NZ)]

    def mask_body(place_ref, counts_ref, a_ref, *outs):
        slot = lax.broadcasted_iota(jnp.int32, (1, width), 1) // HD
        live = (slot < counts_ref[place_ref[3]]).astype(jnp.float32).astype(jnp.bfloat16)
        for q in range(2):
            parity = (place_ref[1] + 1 + q) % NH
            for a in range(NZ):
                outs[q][a * own_rows : (a + 1) * own_rows, :] = (
                    a_ref[block(own_rows, a * NH + parity), :] * live
                )

    act = run(
        mask_body, [of((half, width))] * 2, (place, counts, attn[0]), [SMEM, SMEM, VMEM],
        after=(g_out4[0],), out_specs=[VMEM] * 2, name="mask",
    )
    left = [shift(act[0], 1), None]
    right = [None, shift(act[1], -1)]
    g_far = [swap(g) for g in g_near]

    def join_w(a, b, c, e, out_ref):
        for k, ref in enumerate((a, b, c, e)):
            out_ref[:, k * width : (k + 1) * width] = ref[...]

    w_own = run(
        join_w, of((piece, lanes)), w_near, [VMEM] * NZ, after=(act[0],), name="w_join"
    )

    def move(a_ref, out_ref):
        out_ref[...] = a_ref[...]

    w_pair = run(
        move, of((piece, lanes)), (lax.ppermute(w_own, "dp", pair),), [VMEM],
        after=(left[0], right[1], *g_near[1:], g_far[0]), name="w_move",
    )

    def gather(x):
        return lax.all_gather(x, "dp", axis=0, tiled=True, axis_index_groups=groups)

    w_all = [gather(w_own), gather(w_pair)]

    left[1] = shift(act[1], 1)
    right[0] = shift(act[0], -1)
    across = [shift(left[0], 1), shift(right[1], -1)]
    acts = [*act, *left, *across, *right]

    def join_g(place_ref, *refs):
        for q in range(2):
            for k in range(NZ):
                row = q * NZ + (place_ref[0] + NZ - k) % NZ
                refs[-1][block(own_rows, row), :] = refs[q * NZ + k][...]

    cot = run(
        join_g, of((s, 2 * feats)), (place, *g_far, *g_near), [SMEM] + [VMEM] * (2 * NZ),
        name="g_join",
    )

    tile = min(256, feats)
    steps = feats // tile

    def term_of(i, after):
        def body(g_ref, *refs):
            top, bottom, out_ref = g_ref[:half, :], g_ref[half:, :], refs[-1]
            for k in range(NZ):
                out_ref[:, k * width : (k + 1) * width] = (
                    dot(top, refs[2 * k][...], ((0,), (0,)))
                    + dot(bottom, refs[2 * k + 1][...], ((0,), (0,)))
                ).astype(jnp.bfloat16)

        return run(
            body, of((feats, lanes)), (cot, *acts),
            [pl.BlockSpec((s, tile), lambda j: (0, i * steps + j))] + [VMEM] * 8,
            after=after, grid=(steps,), out_specs=pl.BlockSpec((tile, lanes), lambda j: (j, 0)),
            name="term", limit=BIG,
        )

    def project(i, after):
        def body(w_ref, *refs):
            for q in range(2):
                total = 0.0
                for k in range(NZ):
                    w = w_ref[:, k * width : (k + 1) * width]
                    total += dot(refs[2 * k + q][...], w, ((1,), (1,)))
                refs[8 + q][...] = total.astype(refs[8 + q].dtype)

        return run(
            body, [of((half, feats)), of((half, feats), jnp.float32)], (w_all[i], *acts),
            [pl.BlockSpec((tile, lanes), lambda j: (j, 0))] + [VMEM] * 8,
            after=after, grid=(steps,), out_specs=[pl.BlockSpec((half, tile), lambda j: (0, j))] * 2,
            name="project", limit=BIG,
        )

    cols = width // 3 if width % 384 == 0 else width

    def rows_term(k, dtypes, after):
        def body(g_ref, w_ref, v_ref, *refs):
            total = dot(g_ref[:, :feats], w_ref[...], ((1,), (0,)))
            total += dot(g_ref[:, feats:], v_ref[...], ((1,), (0,)))
            if len(dtypes) == 2:
                refs[0][...] = total[:half].astype(dtypes[0])
                refs[1][...] = total[half:].astype(dtypes[1])
            else:
                refs[0][...] = total.astype(dtypes[0])

        n = width // cols
        outs = [of((s // len(dtypes), width), dtype) for dtype in dtypes]
        column = pl.BlockSpec((feats, cols), lambda j: (0, k * n + j))
        return run(
            body, outs, [cot, w_all[0], w_all[1]], [VMEM, column, column], after=after, grid=(n,),
            out_specs=[pl.BlockSpec((o.shape[0], cols), lambda j: (0, j)) for o in outs],
            name="rows_term", limit=BIG,
        )

    def scatter(x):
        return lax.psum_scatter(
            x, "dp", scatter_dimension=0, tiled=True, axis_index_groups=groups
        )

    term_pair = term_of(1, ())
    term_own = term_of(0, (term_pair,))
    def settle(place_ref, kept_ref, got_ref, *outs):
        for k in range(NZ):
            row = block(own_rows, (place_ref[0] + k) % NZ)
            outs[k][...] = (kept_ref[row, :] + got_ref[row, :].astype(jnp.float32)).astype(
                jnp.bfloat16
            )

    def spread(kept, got, after):
        outs = run(
            settle, [of((own_rows, feats))] * NZ, (place, kept, got), [SMEM, VMEM, VMEM],
            after=after, out_specs=[VMEM] * NZ, name="settle",
        )
        return [outs[0]] + [shift(outs[k], k) for k in range(1, NZ)], outs[0]

    bf16, f32 = jnp.bfloat16, jnp.float32
    far = rows_term(2, (bf16, bf16), (term_own,))
    up = shift(far[0], 1)
    down = shift(far[1], -1)
    sent0, kept0 = project(0, (far[0],))
    got0 = swap(sent0)
    right_top, right_bottom = rows_term(3, (f32, bf16), (sent0,))
    left_top, left_bottom = rows_term(1, (bf16, f32), (right_bottom, up, down))
    from_left_bottom = shift(right_bottom, 1)
    from_right_top = shift(left_top, -1)

    def add_far(a_ref, up_ref, b_ref, down_ref, *outs):
        outs[0][...] = (a_ref[...] + up_ref[...].astype(jnp.float32)).astype(jnp.bfloat16)
        outs[1][...] = (b_ref[...] + down_ref[...].astype(jnp.float32)).astype(jnp.bfloat16)

    right_top, left_bottom = run(
        add_far, [of((half, width))] * 2, (right_top, up, left_bottom, down), [VMEM] * 4,
        after=(left_top,), out_specs=[VMEM] * 2, name="add_far",
    )
    from_left = [shift(right_top, 1), from_left_bottom]
    from_right = [from_right_top, shift(left_bottom, -1)]
    sent1, kept1 = project(1, (right_top,))
    got1 = swap(sent1)
    quarters0, last = spread(kept0, got0, (sent1, from_left_bottom, from_right_top))
    stay = rows_term(0, (f32,), (last,))[0]
    quarters1, last = spread(kept1, got1, (stay, *quarters0[1:]))
    term_pair = run(
        move, of((piece, lanes)), (scatter(term_pair),), [VMEM], after=(stay,), name="move"
    )
    term_pair = lax.ppermute(term_pair, "dp", pair)
    term_own = scatter(term_own)

    def add_rows(place_ref, counts_ref, stay_ref, *refs):
        slot = lax.broadcasted_iota(jnp.int32, (1, width), 1) // HD
        live = (slot < counts_ref[place_ref[3]]).astype(jnp.float32)
        for q in range(2):
            parity = (place_ref[1] + 1 + q) % NH
            for a in range(NZ):
                rows = slice(a * own_rows, (a + 1) * own_rows)
                total = (
                    stay_ref[q * half + a * own_rows : q * half + (a + 1) * own_rows, :]
                    + refs[q][rows, :].astype(jnp.float32)
                    + refs[2 + q][rows, :].astype(jnp.float32)
                )
                refs[4][block(own_rows, a * NH + parity), :] = (total * live).astype(
                    jnp.bfloat16
                )

    grad_rows = run(
        add_rows, of((s, width)), (place, counts, stay, *from_left, *from_right), [SMEM] * 2 + [VMEM] * 5,
        after=(last,), name="add_rows",
    )

    def join_out(place_ref, *refs):
        out_ref = refs[-1]
        for i in range(2):
            first = ((place_ref[2] + i) % 2) * n_x
            for k in range(NZ):
                zk = (place_ref[0] + NZ - k) % NZ
                for x in range(n_x):
                    out_ref[:, block(piece, (first + x) * NZ + zk)] = refs[i * NZ + k][
                        :, x * piece : (x + 1) * piece
                    ]

    projected = run(
        join_out, of((own_rows, d)), (place, *quarters0, *quarters1),
        [SMEM] + [VMEM] * (2 * NZ), name="join_out",
    )

    def add_terms(a_ref, b_ref, *outs):
        for k in range(NZ):
            cols = slice(k * width, (k + 1) * width)
            outs[k][...] = (
                a_ref[:, cols].astype(jnp.float32) + b_ref[:, cols].astype(jnp.float32)
            ).astype(jnp.bfloat16)

    parts = run(
        add_terms, [of((piece, width))] * NZ, (term_own, term_pair), [VMEM] * 2,
        after=(last, grad_rows), out_specs=[VMEM] * NZ, name="add_terms",
    )
    parts = [parts[0]] + [shift(parts[k], -k) for k in range(1, NZ)]

    def join_term(place_ref, *refs):
        for k in range(NZ):
            refs[-1][block(piece, (place_ref[0] + k) % NZ), :] = refs[k][...].astype(
                jnp.float32
            )

    grad_w = run(
        join_term, of((NZ * piece, width), jnp.float32), (place, *parts),
        [SMEM] + [VMEM] * NZ, name="join_term",
    )
    return (projected[None], grad_rows[None], grad_w)


def solution(mesh):
    placed = (P("dp", None, "tensor"), P("dp", "tensor"), P(), P("dp", "tensor", None))
    return jax.shard_map(
        per_device,
        mesh=mesh,
        in_specs=placed,
        out_specs=(P("dp", "tensor", None), P("dp", None, "tensor"), P("dp", "tensor")),
        check_vma=False,
    )
```

```python
import jax
import jax.numpy as jnp
from jax import lax
from jax.experimental import pallas as pl
from jax.experimental.pallas import tpu as pltpu
from jax.sharding import PartitionSpec as P

HD = 128
NZ = 4
NH = 2
SWAP = [(t, t ^ 1) for t in range(NZ * NH)]
ANY = pl.BlockSpec(memory_space=pl.ANY)
SMEM = pl.BlockSpec(memory_space=pltpu.SMEM)
VMEM = pl.BlockSpec(memory_space=pltpu.VMEM)
BIG = 56 << 20
SMALL = 56 << 20


def ring(step):
    return [
        (z * NH + h, ((z + step) % NZ) * NH + h) for z in range(NZ) for h in range(NH)
    ]


def shift(value, step):
    return lax.ppermute(value, "tensor", ring(step))


def swap(value):
    return lax.ppermute(value, "tensor", SWAP)


def dot(a, b, dims):
    return lax.dot_general(a, b, (dims, ((), ())), preferred_element_type=jnp.float32)


def of(shape, dtype=jnp.bfloat16):
    return jax.ShapeDtypeStruct(shape, dtype)


def run(body, out, args, specs, after=(), grid=(), out_specs=VMEM, name=None, limit=SMALL):
    n, m = len(args), len(after)

    def kernel(*refs):
        body(*refs[:n], *refs[n + m :])

    return pl.pallas_call(
        kernel,
        out_shape=out,
        grid=grid,
        in_specs=list(specs) + [ANY] * m,
        out_specs=out_specs,
        name=name,
        cost_estimate=pl.CostEstimate(flops=1000, bytes_accessed=1000, transcendentals=0),
        compiler_params=pltpu.CompilerParams(vmem_limit_bytes=limit),
    )(*args, *after)


def block(rows, start=0):
    return pl.ds(pl.multiple_of(start * rows, rows), rows)


def per_device(attn, w_out, counts, grad_out):
    rank = lax.axis_index("tensor")
    z, h = rank // NH, rank % NH
    s, width = attn.shape[1:]
    own_rows, d = grad_out.shape[1:]
    n_dp = d // w_out.shape[0]
    n_x = n_dp // 2
    piece = w_out.shape[0] // NZ
    feats = n_x * piece
    half = s // 2
    lanes = NZ * width
    y = lax.axis_index("dp") // n_x
    groups = [list(range(n_x)), list(range(n_x, n_dp))]
    pair = [(i, (i + n_x) % n_dp) for i in range(n_dp)]
    place = jnp.stack([z, h, y, rank]).astype(jnp.int32)

    def split_w(place_ref, w_ref, *outs):
        for k in range(NZ):
            outs[k][...] = w_ref[block(piece, (place_ref[0] + k) % NZ), :]

    w_out4 = run(
        split_w, [of((piece, width))] * NZ, (place, w_out), [SMEM, VMEM],
        out_specs=[VMEM] * NZ, name="w_split",
    )
    w_near = [w_out4[0]] + [shift(w_out4[k], k) for k in range(1, NZ)]

    def split_g(place_ref, g_ref, *outs):
        for k in range(NZ):
            zk = (place_ref[0] + k) % NZ
            for i in range(2):
                first = ((place_ref[2] + i) % 2) * n_x
                for x in range(n_x):
                    outs[k][:, (i * n_x + x) * piece : (i * n_x + x + 1) * piece] = g_ref[
                        :, block(piece, (first + x) * NZ + zk)
                    ]

    g_out4 = run(
        split_g, [of((own_rows, 2 * feats))] * NZ, (place, grad_out[0]), [SMEM, VMEM],
        after=(w_out4[0],), out_specs=[VMEM] * NZ, name="g_split",
    )
    g_near = [g_out4[0]] + [shift(g_out4[k], k) for k in range(1, NZ)]

    def mask_body(place_ref, counts_ref, a_ref, *outs):
        slot = lax.broadcasted_iota(jnp.int32, (1, width), 1) // HD
        live = (slot < counts_ref[place_ref[3]]).astype(jnp.float32).astype(jnp.bfloat16)
        for q in range(2):
            parity = (place_ref[1] + 1 + q) % NH
            for a in range(NZ):
                outs[q][a * own_rows : (a + 1) * own_rows, :] = (
                    a_ref[block(own_rows, a * NH + parity), :] * live
                )

    act = run(
        mask_body, [of((half, width))] * 2, (place, counts, attn[0]), [SMEM, SMEM, VMEM],
        after=(g_out4[0],), out_specs=[VMEM] * 2, name="mask",
    )
    left = [shift(act[0], 1), None]
    right = [None, shift(act[1], -1)]
    g_far = [swap(g) for g in g_near]

    def join_w(a, b, c, e, out_ref):
        for k, ref in enumerate((a, b, c, e)):
            out_ref[:, k * width : (k + 1) * width] = ref[...]

    w_own = run(
        join_w, of((piece, lanes)), w_near, [VMEM] * NZ, after=(act[0],), name="w_join"
    )

    def move(a_ref, out_ref):
        out_ref[...] = a_ref[...]

    w_pair = run(
        move, of((piece, lanes)), (lax.ppermute(w_own, "dp", pair),), [VMEM],
        after=(left[0], right[1], *g_near[1:], g_far[0]), name="w_move",
    )

    def gather(x):
        return lax.all_gather(x, "dp", axis=0, tiled=True, axis_index_groups=groups)

    w_all = [gather(w_own), gather(w_pair)]

    left[1] = shift(act[1], 1)
    right[0] = shift(act[0], -1)
    across = [shift(left[0], 1), shift(right[1], -1)]
    acts = [*act, *left, *across, *right]

    def join_g(place_ref, *refs):
        for q in range(2):
            for k in range(NZ):
                row = q * NZ + (place_ref[0] + NZ - k) % NZ
                refs[-1][block(own_rows, row), :] = refs[q * NZ + k][...]

    cot = run(
        join_g, of((s, 2 * feats)), (place, *g_far, *g_near), [SMEM] + [VMEM] * (2 * NZ),
        name="g_join",
    )

    tile = min(256, feats)
    steps = feats // tile

    def term_of(i, after):
        def body(g_ref, *refs):
            top, bottom, out_ref = g_ref[:half, :], g_ref[half:, :], refs[-1]
            for k in range(NZ):
                out_ref[:, k * width : (k + 1) * width] = (
                    dot(top, refs[2 * k][...], ((0,), (0,)))
                    + dot(bottom, refs[2 * k + 1][...], ((0,), (0,)))
                ).astype(jnp.bfloat16)

        return run(
            body, of((feats, lanes)), (cot, *acts),
            [pl.BlockSpec((s, tile), lambda j: (0, i * steps + j))] + [VMEM] * 8,
            after=after, grid=(steps,), out_specs=pl.BlockSpec((tile, lanes), lambda j: (j, 0)),
            name="term", limit=BIG,
        )

    def project(i, cuts, after):
        part = half // cuts

        def body(w_ref, *refs):
            for q in range(2):
                total = 0.0
                for k in range(NZ):
                    w = w_ref[:, k * width : (k + 1) * width]
                    total += dot(refs[2 * k + q][...], w, ((1,), (1,)))
                if q:
                    refs[8 + cuts][...] = total
                else:
                    for p in range(cuts):
                        refs[8 + p][...] = total[p * part : (p + 1) * part].astype(jnp.bfloat16)

        return run(
            body, [of((part, feats))] * cuts + [of((half, feats), jnp.float32)], (w_all[i], *acts),
            [pl.BlockSpec((tile, lanes), lambda j: (j, 0))] + [VMEM] * 8,
            after=after, grid=(steps,), out_specs=[pl.BlockSpec((r, tile), lambda j: (0, j)) for r in [part] * cuts + [half]],
            name="project", limit=BIG,
        )

    cols = width // 3 if width % 384 == 0 else width

    def rows_term(k, dtypes, after):
        def body(g_ref, w_ref, v_ref, *refs):
            total = dot(g_ref[:, :feats], w_ref[...], ((1,), (0,)))
            total += dot(g_ref[:, feats:], v_ref[...], ((1,), (0,)))
            if len(dtypes) == 2:
                refs[0][...] = total[:half].astype(dtypes[0])
                refs[1][...] = total[half:].astype(dtypes[1])
            else:
                refs[0][...] = total.astype(dtypes[0])

        n = width // cols
        outs = [of((s // len(dtypes), width), dtype) for dtype in dtypes]
        column = pl.BlockSpec((feats, cols), lambda j: (0, k * n + j))
        return run(
            body, outs, [cot, w_all[0], w_all[1]], [VMEM, column, column], after=after, grid=(n,),
            out_specs=[pl.BlockSpec((o.shape[0], cols), lambda j: (0, j)) for o in outs],
            name="rows_term", limit=BIG,
        )

    def scatter(x):
        return lax.psum_scatter(
            x, "dp", scatter_dimension=0, tiled=True, axis_index_groups=groups
        )

    def settle(place_ref, kept_ref, *refs):
        got, outs = refs[:-NZ], refs[-NZ:]
        near = NZ // len(got)
        for k in range(NZ):
            zk = (place_ref[0] + k) % NZ
            row = block(own_rows, zk % near)
            total = got[0][row, :].astype(jnp.float32)
            if len(got) == 2:
                total = jnp.where(zk < near, total, got[1][row, :].astype(jnp.float32))
            outs[k][...] = (kept_ref[block(own_rows, zk), :] + total).astype(jnp.bfloat16)

    def spread(kept, got, after):
        outs = run(
            settle, [of((own_rows, feats))] * NZ, (place, kept, *got), [SMEM] + [VMEM] * (1 + len(got)),
            after=after, out_specs=[VMEM] * NZ, name="settle",
        )
        return [outs[0]] + [shift(outs[k], k) for k in range(1, NZ)], outs[0]

    bf16, f32 = jnp.bfloat16, jnp.float32
    *sent0, kept0 = project(0, 1, ())
    got0 = [swap(x) for x in sent0]
    term_pair = term_of(1, (kept0,))
    far = rows_term(2, (bf16, bf16), (term_pair,))
    up = shift(far[0], 1)
    down = shift(far[1], -1)
    right_top, right_bottom = rows_term(3, (f32, bf16), (far[0],))
    left_top, left_bottom = rows_term(1, (bf16, f32), (right_bottom,))
    from_left_bottom = shift(right_bottom, 1)
    from_right_top = shift(left_top, -1)
    stay = rows_term(0, (f32,), (left_top,))[0]
    term_own = term_of(0, (stay, *got0, up, down))

    def add_far(a_ref, up_ref, b_ref, down_ref, *outs):
        outs[0][...] = (a_ref[...] + up_ref[...].astype(jnp.float32)).astype(jnp.bfloat16)
        outs[1][...] = (b_ref[...] + down_ref[...].astype(jnp.float32)).astype(jnp.bfloat16)

    right_top, left_bottom = run(
        add_far, [of((half, width))] * 2, (right_top, up, left_bottom, down), [VMEM] * 4,
        after=(term_own,), out_specs=[VMEM] * 2, name="add_far",
    )
    from_left = [shift(right_top, 1), from_left_bottom]
    from_right = [from_right_top, shift(left_bottom, -1)]
    quarters0, last = spread(kept0, got0, (right_top,))
    *sent1, kept1 = project(1, 2, (last,))
    got1 = [swap(x) for x in sent1]
    term_pair = lax.ppermute(scatter(term_pair), "dp", pair)
    term_own = scatter(term_own)

    def add_rows(place_ref, counts_ref, stay_ref, *refs):
        slot = lax.broadcasted_iota(jnp.int32, (1, width), 1) // HD
        live = (slot < counts_ref[place_ref[3]]).astype(jnp.float32)
        for q in range(2):
            parity = (place_ref[1] + 1 + q) % NH
            for a in range(NZ):
                rows = slice(a * own_rows, (a + 1) * own_rows)
                total = (
                    stay_ref[q * half + a * own_rows : q * half + (a + 1) * own_rows, :]
                    + refs[q][rows, :].astype(jnp.float32)
                    + refs[2 + q][rows, :].astype(jnp.float32)
                )
                refs[4][block(own_rows, a * NH + parity), :] = (total * live).astype(
                    jnp.bfloat16
                )

    grad_rows = run(
        add_rows, of((s, width)), (place, counts, stay, *from_left, *from_right), [SMEM] * 2 + [VMEM] * 5,
        name="add_rows",
    )
    quarters1, last = spread(kept1, got1, (grad_rows,))

    def join_out(place_ref, *refs):
        out_ref = refs[-1]
        for i in range(2):
            first = ((place_ref[2] + i) % 2) * n_x
            for k in range(NZ):
                zk = (place_ref[0] + NZ - k) % NZ
                for x in range(n_x):
                    out_ref[:, block(piece, (first + x) * NZ + zk)] = refs[i * NZ + k][
                        :, x * piece : (x + 1) * piece
                    ]

    projected = run(
        join_out, of((own_rows, d)), (place, *quarters0, *quarters1),
        [SMEM] + [VMEM] * (2 * NZ), name="join_out",
    )

    def add_terms(a_ref, b_ref, *outs):
        for k in range(NZ):
            cols = slice(k * width, (k + 1) * width)
            outs[k][...] = (
                a_ref[:, cols].astype(jnp.float32) + b_ref[:, cols].astype(jnp.float32)
            ).astype(jnp.bfloat16)

    parts = run(
        add_terms, [of((piece, width))] * NZ, (term_own, term_pair), [VMEM] * 2,
        after=(last, *quarters0[1:]), out_specs=[VMEM] * NZ, name="add_terms",
    )
    parts = [parts[0]] + [shift(parts[k], -k) for k in range(1, NZ)]

    def join_term(place_ref, *refs):
        for k in range(NZ):
            refs[-1][block(piece, (place_ref[0] + k) % NZ), :] = refs[k][...].astype(
                jnp.float32
            )

    grad_w = run(
        join_term, of((NZ * piece, width), jnp.float32), (place, *parts),
        [SMEM] + [VMEM] * NZ, name="join_term",
    )
    return (projected[None], grad_rows[None], grad_w)


def solution(mesh):
    placed = (P("dp", None, "tensor"), P("dp", "tensor"), P(), P("dp", "tensor", None))
    return jax.shard_map(
        per_device,
        mesh=mesh,
        in_specs=placed,
        out_specs=(P("dp", "tensor", None), P("dp", None, "tensor"), P("dp", "tensor")),
        check_vma=False,
    )
```

```python
import jax
import jax.numpy as jnp
from jax import lax
from jax.experimental import pallas as pl
from jax.experimental.pallas import tpu as pltpu
from jax.sharding import PartitionSpec as P

HD = 128
NZ = 4
NH = 2
SWAP = [(t, t ^ 1) for t in range(NZ * NH)]
ANY = pl.BlockSpec(memory_space=pl.ANY)
SMEM = pl.BlockSpec(memory_space=pltpu.SMEM)
VMEM = pl.BlockSpec(memory_space=pltpu.VMEM)
BIG = 56 << 20
SMALL = 56 << 20


def ring(step):
    return [
        (z * NH + h, ((z + step) % NZ) * NH + h) for z in range(NZ) for h in range(NH)
    ]


def shift(value, step):
    return lax.ppermute(value, "tensor", ring(step))


def swap(value):
    return lax.ppermute(value, "tensor", SWAP)


def dot(a, b, dims):
    return lax.dot_general(a, b, (dims, ((), ())), preferred_element_type=jnp.float32)


def of(shape, dtype=jnp.bfloat16):
    return jax.ShapeDtypeStruct(shape, dtype)


def run(body, out, args, specs, after=(), grid=(), out_specs=VMEM, name=None, limit=SMALL):
    n, m = len(args), len(after)

    def kernel(*refs):
        body(*refs[:n], *refs[n + m :])

    return pl.pallas_call(
        kernel,
        out_shape=out,
        grid=grid,
        in_specs=list(specs) + [ANY] * m,
        out_specs=out_specs,
        name=name,
        cost_estimate=pl.CostEstimate(flops=1000, bytes_accessed=1000, transcendentals=0),
        compiler_params=pltpu.CompilerParams(vmem_limit_bytes=limit),
    )(*args, *after)


def block(rows, start=0):
    return pl.ds(pl.multiple_of(start * rows, rows), rows)


def per_device(attn, w_out, counts, grad_out):
    rank = lax.axis_index("tensor")
    z, h = rank // NH, rank % NH
    s, width = attn.shape[1:]
    own_rows, d = grad_out.shape[1:]
    n_dp = d // w_out.shape[0]
    n_x = n_dp // 2
    piece = w_out.shape[0] // NZ
    feats = n_x * piece
    half = s // 2
    lanes = NZ * width
    y = lax.axis_index("dp") // n_x
    groups = [list(range(n_x)), list(range(n_x, n_dp))]
    pair = [(i, (i + n_x) % n_dp) for i in range(n_dp)]
    place = jnp.stack([z, h, y, rank]).astype(jnp.int32)

    def split_w(place_ref, w_ref, *outs):
        for k in range(NZ):
            outs[k][...] = w_ref[block(piece, (place_ref[0] + k) % NZ), :]

    w_out4 = run(
        split_w, [of((piece, width))] * NZ, (place, w_out), [SMEM, VMEM],
        out_specs=[VMEM] * NZ, name="w_split",
    )
    w_near = [w_out4[0]] + [shift(w_out4[k], k) for k in range(1, NZ)]

    def split_g(place_ref, g_ref, *outs):
        for k in range(NZ):
            zk = (place_ref[0] + k) % NZ
            for i in range(2):
                first = ((place_ref[2] + i) % 2) * n_x
                for x in range(n_x):
                    outs[k][:, (i * n_x + x) * piece : (i * n_x + x + 1) * piece] = g_ref[
                        :, block(piece, (first + x) * NZ + zk)
                    ]

    g_out4 = run(
        split_g, [of((own_rows, 2 * feats))] * NZ, (place, grad_out[0]), [SMEM, VMEM],
        after=(w_out4[0],), out_specs=[VMEM] * NZ, name="g_split",
    )
    g_near = [g_out4[0]] + [shift(g_out4[k], k) for k in range(1, NZ)]

    def mask_body(place_ref, counts_ref, a_ref, *outs):
        slot = lax.broadcasted_iota(jnp.int32, (1, width), 1) // HD
        live = (slot < counts_ref[place_ref[3]]).astype(jnp.float32).astype(jnp.bfloat16)
        for q in range(2):
            parity = (place_ref[1] + 1 + q) % NH
            for a in range(NZ):
                outs[q][a * own_rows : (a + 1) * own_rows, :] = (
                    a_ref[block(own_rows, a * NH + parity), :] * live
                )

    act = run(
        mask_body, [of((half, width))] * 2, (place, counts, attn[0]), [SMEM, SMEM, VMEM],
        after=(g_out4[0],), out_specs=[VMEM] * 2, name="mask",
    )
    left = [shift(act[0], 1), None]
    right = [None, shift(act[1], -1)]
    g_far = [swap(g) for g in g_near]

    def join_w(a, b, c, e, out_ref):
        for k, ref in enumerate((a, b, c, e)):
            out_ref[:, k * width : (k + 1) * width] = ref[...]

    w_own = run(
        join_w, of((piece, lanes)), w_near, [VMEM] * NZ, after=(act[0],), name="w_join"
    )

    def move(a_ref, out_ref):
        out_ref[...] = a_ref[...]

    w_pair = run(
        move, of((piece, lanes)), (lax.ppermute(w_own, "dp", pair),), [VMEM],
        after=(left[0], right[1], *g_near[1:], g_far[0]), name="w_move",
    )

    def gather(x):
        return lax.all_gather(x, "dp", axis=0, tiled=True, axis_index_groups=groups)

    w_all = [gather(w_own), gather(w_pair)]

    left[1] = shift(act[1], 1)
    right[0] = shift(act[0], -1)
    across = [shift(left[0], 1), shift(right[1], -1)]
    acts = [*act, *left, *across, *right]

    def join_g(place_ref, *refs):
        for q in range(2):
            for k in range(NZ):
                row = q * NZ + (place_ref[0] + NZ - k) % NZ
                refs[-1][block(own_rows, row), :] = refs[q * NZ + k][...]

    cot = run(
        join_g, of((s, 2 * feats)), (place, *g_far, *g_near), [SMEM] + [VMEM] * (2 * NZ),
        name="g_join",
    )

    tile = min(256, feats)
    steps = feats // tile

    def term_of(i, after):
        def body(g_ref, *refs):
            top, bottom, out_ref = g_ref[:half, :], g_ref[half:, :], refs[-1]
            for k in range(NZ):
                out_ref[:, k * width : (k + 1) * width] = (
                    dot(top, refs[2 * k][...], ((0,), (0,)))
                    + dot(bottom, refs[2 * k + 1][...], ((0,), (0,)))
                ).astype(jnp.bfloat16)

        return run(
            body, of((feats, lanes)), (cot, *acts),
            [pl.BlockSpec((s, tile), lambda j: (0, i * steps + j))] + [VMEM] * 8,
            after=after, grid=(steps,), out_specs=pl.BlockSpec((tile, lanes), lambda j: (j, 0)),
            name="term", limit=BIG,
        )

    def project(i, cuts, after):
        part = half // cuts

        def body(w_ref, *refs):
            for q in range(2):
                total = 0.0
                for k in range(NZ):
                    w = w_ref[:, k * width : (k + 1) * width]
                    total += dot(refs[2 * k + q][...], w, ((1,), (1,)))
                if q:
                    refs[8 + cuts][...] = total
                else:
                    for p in range(cuts):
                        refs[8 + p][...] = total[p * part : (p + 1) * part].astype(jnp.bfloat16)

        return run(
            body, [of((part, feats))] * cuts + [of((half, feats), jnp.float32)], (w_all[i], *acts),
            [pl.BlockSpec((tile, lanes), lambda j: (j, 0))] + [VMEM] * 8,
            after=after, grid=(steps,), out_specs=[pl.BlockSpec((r, tile), lambda j: (0, j)) for r in [part] * cuts + [half]],
            name="project", limit=BIG,
        )

    cols = width // 3 if width % 384 == 0 else width

    def rows_term(k, dtypes, after, more=(), q=0):
        def body(g_ref, w_ref, v_ref, *refs):
            total = dot(g_ref[:, :feats], w_ref[...], ((1,), (0,)))
            total += dot(g_ref[:, feats:], v_ref[...], ((1,), (0,)))
            if len(dtypes) == 2:
                refs[0][...] = total[:half].astype(dtypes[0])
                refs[1][...] = total[half:].astype(dtypes[1])
            elif more:
                parts = [total[:half], total[half:]]
                parts[q] += refs[0][...].astype(jnp.float32)
                refs[1][:half, :] = parts[0].astype(dtypes[0])
                refs[1][half:, :] = parts[1].astype(dtypes[0])
            else:
                refs[0][...] = total.astype(dtypes[0])

        n = width // cols
        outs = [of((s // len(dtypes), width), dtype) for dtype in dtypes]
        column = pl.BlockSpec((feats, cols), lambda j: (0, k * n + j))
        return run(
            body, outs, [cot, w_all[0], w_all[1], *more],
            [VMEM, column, column] + [pl.BlockSpec((half, cols), lambda j: (0, j))] * len(more),
            after=after, grid=(n,),
            out_specs=[pl.BlockSpec((o.shape[0], cols), lambda j: (0, j)) for o in outs],
            name="rows_term", limit=BIG,
        )

    def scatter(x):
        return lax.psum_scatter(
            x, "dp", scatter_dimension=0, tiled=True, axis_index_groups=groups
        )

    def settle(place_ref, kept_ref, *refs):
        got, outs = refs[:-NZ], refs[-NZ:]
        near = NZ // len(got)
        for k in range(NZ):
            zk = (place_ref[0] + k) % NZ
            row = block(own_rows, zk % near)
            total = got[0][row, :].astype(jnp.float32)
            if len(got) == 2:
                total = jnp.where(zk < near, total, got[1][row, :].astype(jnp.float32))
            outs[k][...] = (kept_ref[block(own_rows, zk), :] + total).astype(jnp.bfloat16)

    def spread(kept, got, after):
        outs = run(
            settle, [of((own_rows, feats))] * NZ, (place, kept, *got), [SMEM] + [VMEM] * (1 + len(got)),
            after=after, out_specs=[VMEM] * NZ, name="settle",
        )
        return [outs[0]] + [shift(outs[k], k) for k in range(1, NZ)], outs[0]

    bf16, f32 = jnp.bfloat16, jnp.float32
    term_pair = term_of(1, ())
    term_own = term_of(0, (term_pair,))
    far = rows_term(2, (bf16, bf16), (term_own,))
    up = shift(far[0], 1)
    down = shift(far[1], -1)
    *sent0, kept0 = project(0, 1, (far[0],))
    got0 = [swap(x) for x in sent0]
    to_right = rows_term(3, (bf16,), (kept0,), (up,), 0)[0]
    to_left = rows_term(1, (bf16,), (to_right,), (down,), 1)[0]
    from_left = shift(to_right, 1)
    from_right = shift(to_left, -1)
    stay = rows_term(0, (f32,), (to_left,))[0]
    term_pair = run(
        move, of((piece, lanes)), (scatter(term_pair),), [VMEM], after=(stay,), name="move"
    )
    *sent1, kept1 = project(1, 1, (stay, term_pair, *got0))
    got1 = [swap(x) for x in sent1]
    quarters0, last = spread(kept0, got0, (kept1,))
    term_pair = lax.ppermute(term_pair, "dp", pair)
    term_own = scatter(term_own)

    def add_rows(place_ref, counts_ref, stay_ref, *refs):
        slot = lax.broadcasted_iota(jnp.int32, (1, width), 1) // HD
        live = (slot < counts_ref[place_ref[3]]).astype(jnp.float32)
        for q in range(2):
            parity = (place_ref[1] + 1 + q) % NH
            for a in range(NZ):
                row = q * half + a * own_rows
                rows = slice(row, row + own_rows)
                total = (
                    stay_ref[rows, :]
                    + refs[0][rows, :].astype(jnp.float32)
                    + refs[1][rows, :].astype(jnp.float32)
                )
                refs[2][block(own_rows, a * NH + parity), :] = (total * live).astype(
                    jnp.bfloat16
                )

    grad_rows = run(
        add_rows, of((s, width)), (place, counts, stay, from_left, from_right), [SMEM] * 2 + [VMEM] * 3,
        name="add_rows",
    )
    quarters1, last = spread(kept1, got1, (grad_rows,))

    def join_out(place_ref, *refs):
        out_ref = refs[-1]
        for i in range(2):
            first = ((place_ref[2] + i) % 2) * n_x
            for k in range(NZ):
                zk = (place_ref[0] + NZ - k) % NZ
                for x in range(n_x):
                    out_ref[:, block(piece, (first + x) * NZ + zk)] = refs[i * NZ + k][
                        :, x * piece : (x + 1) * piece
                    ]

    projected = run(
        join_out, of((own_rows, d)), (place, *quarters0, *quarters1),
        [SMEM] + [VMEM] * (2 * NZ), name="join_out",
    )

    def add_terms(a_ref, b_ref, *outs):
        for k in range(NZ):
            cols = slice(k * width, (k + 1) * width)
            outs[k][...] = (
                a_ref[:, cols].astype(jnp.float32) + b_ref[:, cols].astype(jnp.float32)
            ).astype(jnp.bfloat16)

    parts = run(
        add_terms, [of((piece, width))] * NZ, (term_own, term_pair), [VMEM] * 2,
        after=(last, *quarters0[1:]), out_specs=[VMEM] * NZ, name="add_terms",
    )
    parts = [parts[0]] + [shift(parts[k], -k) for k in range(1, NZ)]

    def join_term(place_ref, *refs):
        for k in range(NZ):
            refs[-1][block(piece, (place_ref[0] + k) % NZ), :] = refs[k][...].astype(
                jnp.float32
            )

    grad_w = run(
        join_term, of((NZ * piece, width), jnp.float32), (place, *parts),
        [SMEM] + [VMEM] * NZ, after=(projected,), name="join_term",
    )
    return (projected[None], grad_rows[None], grad_w)


def solution(mesh):
    placed = (P("dp", None, "tensor"), P("dp", "tensor"), P(), P("dp", "tensor", None))
    return jax.shard_map(
        per_device,
        mesh=mesh,
        in_specs=placed,
        out_specs=(P("dp", "tensor", None), P("dp", None, "tensor"), P("dp", "tensor")),
        check_vma=False,
    )
```

```python
import jax
import jax.numpy as jnp
from jax import lax
from jax.experimental import pallas as pl
from jax.experimental.pallas import tpu as pltpu
from jax.sharding import PartitionSpec as P

HD = 128
NZ = 4
NH = 2
SWAP = [(t, t ^ 1) for t in range(NZ * NH)]
ANY = pl.BlockSpec(memory_space=pl.ANY)
SMEM = pl.BlockSpec(memory_space=pltpu.SMEM)
VMEM = pl.BlockSpec(memory_space=pltpu.VMEM)
BIG = 56 << 20
SMALL = 32 << 20


def ring(step):
    return [
        (z * NH + h, ((z + step) % NZ) * NH + h) for z in range(NZ) for h in range(NH)
    ]


def shift(value, step):
    return lax.ppermute(value, "tensor", ring(step))


def swap(value):
    return lax.ppermute(value, "tensor", SWAP)


def dot(a, b, dims):
    return lax.dot_general(a, b, (dims, ((), ())), preferred_element_type=jnp.float32)


def of(shape, dtype=jnp.bfloat16):
    return jax.ShapeDtypeStruct(shape, dtype)


def run(body, out, args, specs, after=(), grid=(), out_specs=VMEM, name=None, limit=BIG):
    n, m = len(args), len(after)

    def kernel(*refs):
        body(*refs[:n], *refs[n + m :])

    return pl.pallas_call(
        kernel,
        out_shape=out,
        grid=grid,
        in_specs=list(specs) + [ANY] * m,
        out_specs=out_specs,
        name=name,
        cost_estimate=pl.CostEstimate(flops=1000, bytes_accessed=1000, transcendentals=0),
        compiler_params=pltpu.CompilerParams(vmem_limit_bytes=limit),
    )(*args, *after)


def block(rows, start=0):
    return pl.ds(pl.multiple_of(start * rows, rows), rows)


def per_device(attn, w_out, counts, grad_out):
    rank = lax.axis_index("tensor")
    z, h = rank // NH, rank % NH
    s, width = attn.shape[1:]
    own_rows, d = grad_out.shape[1:]
    n_dp = d // w_out.shape[0]
    n_x = n_dp // 2
    piece = w_out.shape[0] // NZ
    feats = n_x * piece
    half = s // 2
    lanes = NZ * width
    y = lax.axis_index("dp") // n_x
    groups = [list(range(n_x)), list(range(n_x, n_dp))]
    pair = [(i, (i + n_x) % n_dp) for i in range(n_dp)]
    place = jnp.stack([z, h, y, rank]).astype(jnp.int32)

    def split_w(place_ref, w_ref, *outs):
        for k in range(NZ):
            outs[k][...] = w_ref[block(piece, (place_ref[0] + k) % NZ), :]

    w_out4 = run(
        split_w, [of((piece, width))] * NZ, (place, w_out), [SMEM, VMEM],
        out_specs=[VMEM] * NZ, name="w_split", limit=SMALL,
    )
    w_near = [w_out4[0]] + [shift(w_out4[k], k) for k in range(1, NZ)]

    def split_g(place_ref, g_ref, *outs):
        for k in range(NZ):
            zk = (place_ref[0] + k) % NZ
            for i in range(2):
                first = ((place_ref[2] + i) % 2) * n_x
                for x in range(n_x):
                    outs[k][:, (i * n_x + x) * piece : (i * n_x + x + 1) * piece] = g_ref[
                        :, block(piece, (first + x) * NZ + zk)
                    ]

    g_out4 = run(
        split_g, [of((own_rows, 2 * feats))] * NZ, (place, grad_out[0]), [SMEM, VMEM],
        after=(w_out4[0],), out_specs=[VMEM] * NZ, name="g_split", limit=SMALL,
    )
    g_near = [g_out4[0]] + [shift(g_out4[k], k) for k in range(1, NZ)]

    def mask_body(place_ref, counts_ref, a_ref, *outs):
        slot = lax.broadcasted_iota(jnp.int32, (1, width), 1) // HD
        live = (slot < counts_ref[place_ref[3]]).astype(jnp.float32).astype(jnp.bfloat16)
        for q in range(2):
            parity = (place_ref[1] + 1 + q) % NH
            for a in range(NZ):
                outs[q][a * own_rows : (a + 1) * own_rows, :] = (
                    a_ref[block(own_rows, a * NH + parity), :] * live
                )

    act = run(
        mask_body, [of((half, width))] * 2, (place, counts, attn[0]), [SMEM, SMEM, VMEM],
        after=(g_out4[0],), out_specs=[VMEM] * 2, name="mask", limit=SMALL,
    )
    left = [shift(act[0], 1), None]
    right = [None, shift(act[1], -1)]
    g_far = [swap(g) for g in g_near]

    def join_w(a, b, c, e, out_ref):
        for k, ref in enumerate((a, b, c, e)):
            out_ref[:, k * width : (k + 1) * width] = ref[...]

    w_own = run(
        join_w, of((piece, lanes)), w_near, [VMEM] * NZ, after=(act[0],), name="w_join", limit=SMALL
    )

    def move(a_ref, out_ref):
        out_ref[...] = a_ref[...]

    w_pair = run(
        move, of((piece, lanes)), (lax.ppermute(w_own, "dp", pair),), [VMEM],
        after=(left[0], right[1], *g_near[1:], g_far[0]), name="w_move",
    )

    def gather(x):
        return lax.all_gather(x, "dp", axis=0, tiled=True, axis_index_groups=groups)

    w_all = [gather(w_own), gather(w_pair)]

    left[1] = shift(act[1], 1)
    right[0] = shift(act[0], -1)
    across = [shift(left[0], 1), shift(right[1], -1)]
    acts = [*act, *left, *across, *right]

    def join_g(place_ref, *refs):
        for q in range(2):
            for k in range(NZ):
                row = q * NZ + (place_ref[0] + NZ - k) % NZ
                refs[-1][block(own_rows, row), :] = refs[q * NZ + k][...]

    cot = run(
        join_g, of((s, 2 * feats)), (place, *g_far, *g_near), [SMEM] + [VMEM] * (2 * NZ),
        name="g_join",
    )

    tile = min(256, feats)
    steps = feats // tile

    def term_of(i, after):
        def body(g_ref, *refs):
            top, bottom, out_ref = g_ref[:half, :], g_ref[half:, :], refs[-1]
            for k in range(NZ):
                out_ref[:, k * width : (k + 1) * width] = (
                    dot(top, refs[2 * k][...], ((0,), (0,)))
                    + dot(bottom, refs[2 * k + 1][...], ((0,), (0,)))
                ).astype(jnp.bfloat16)

        return run(
            body, of((feats, lanes)), (cot, *acts),
            [pl.BlockSpec((s, tile), lambda j: (0, i * steps + j))] + [VMEM] * 8,
            after=after, grid=(steps,), out_specs=pl.BlockSpec((tile, lanes), lambda j: (j, 0)),
            name="term", limit=BIG,
        )

    def project(i, cuts, after):
        part = half // cuts

        def body(w_ref, *refs):
            for q in range(2):
                total = 0.0
                for k in range(NZ):
                    w = w_ref[:, k * width : (k + 1) * width]
                    total += dot(refs[2 * k + q][...], w, ((1,), (1,)))
                if q:
                    refs[8 + cuts][...] = total
                else:
                    for p in range(cuts):
                        refs[8 + p][...] = total[p * part : (p + 1) * part].astype(jnp.bfloat16)

        return run(
            body, [of((part, feats))] * cuts + [of((half, feats), jnp.float32)], (w_all[i], *acts),
            [pl.BlockSpec((tile, lanes), lambda j: (j, 0))] + [VMEM] * 8,
            after=after, grid=(steps,), out_specs=[pl.BlockSpec((r, tile), lambda j: (0, j)) for r in [part] * cuts + [half]],
            name="project", limit=BIG,
        )

    cols = width // 3 if width % 384 == 0 else width

    def rows_term(k, dtypes, after, more=(), q=0):
        def body(g_ref, w_ref, v_ref, *refs):
            total = dot(g_ref[:, :feats], w_ref[...], ((1,), (0,)))
            total += dot(g_ref[:, feats:], v_ref[...], ((1,), (0,)))
            if len(dtypes) == 2:
                refs[0][...] = total[:half].astype(dtypes[0])
                refs[1][...] = total[half:].astype(dtypes[1])
            elif more:
                parts = [total[:half], total[half:]]
                parts[q] += refs[0][...].astype(jnp.float32)
                refs[1][:half, :] = parts[0].astype(dtypes[0])
                refs[1][half:, :] = parts[1].astype(dtypes[0])
            else:
                refs[0][...] = total.astype(dtypes[0])

        n = width // cols
        outs = [of((s // len(dtypes), width), dtype) for dtype in dtypes]
        column = pl.BlockSpec((feats, cols), lambda j: (0, k * n + j))
        return run(
            body, outs, [cot, w_all[0], w_all[1], *more],
            [VMEM, column, column] + [pl.BlockSpec((half, cols), lambda j: (0, j))] * len(more),
            after=after, grid=(n,),
            out_specs=[pl.BlockSpec((o.shape[0], cols), lambda j: (0, j)) for o in outs],
            name="rows_term", limit=BIG,
        )

    def scatter(x):
        return lax.psum_scatter(
            x, "dp", scatter_dimension=0, tiled=True, axis_index_groups=groups
        )

    def settle(place_ref, kept_ref, *refs):
        got, outs = refs[:-NZ], refs[-NZ:]
        near = NZ // len(got)
        for k in range(NZ):
            zk = (place_ref[0] + k) % NZ
            row = block(own_rows, zk % near)
            total = got[0][row, :].astype(jnp.float32)
            if len(got) == 2:
                total = jnp.where(zk < near, total, got[1][row, :].astype(jnp.float32))
            outs[k][...] = (kept_ref[block(own_rows, zk), :] + total).astype(jnp.bfloat16)

    def spread(kept, got, after):
        outs = run(
            settle, [of((own_rows, feats))] * NZ, (place, kept, *got), [SMEM] + [VMEM] * (1 + len(got)),
            after=after, out_specs=[VMEM] * NZ, name="settle",
        )
        return [outs[0]] + [shift(outs[k], k) for k in range(1, NZ)], outs[0]

    bf16, f32 = jnp.bfloat16, jnp.float32
    term_pair = term_of(1, ())
    term_own = term_of(0, (term_pair,))
    far = rows_term(2, (bf16, bf16), (term_own,))
    up = shift(far[0], 1)
    down = shift(far[1], -1)
    *sent0, kept0 = project(0, 1, (far[0],))
    got0 = [swap(x) for x in sent0]
    to_right = rows_term(3, (bf16,), (kept0,), (up,), 0)[0]
    term_pair = run(
        move, of((piece, lanes)), (scatter(term_pair),), [VMEM], after=(to_right,), name="move"
    )
    to_left = rows_term(1, (bf16,), (to_right, term_pair), (down,), 1)[0]
    term_pair = lax.ppermute(term_pair, "dp", pair)
    from_left = shift(to_right, 1)
    from_right = shift(to_left, -1)
    *sent1, kept1 = project(1, 1, (to_left, *got0))
    got1 = [swap(x) for x in sent1]
    stay = rows_term(0, (f32,), (kept1,))[0]
    quarters0, last = spread(kept0, got0, (stay,))
    term_own = scatter(term_own)

    def add_rows(place_ref, counts_ref, stay_ref, *refs):
        slot = lax.broadcasted_iota(jnp.int32, (1, width), 1) // HD
        live = (slot < counts_ref[place_ref[3]]).astype(jnp.float32)
        for q in range(2):
            parity = (place_ref[1] + 1 + q) % NH
            for a in range(NZ):
                row = q * half + a * own_rows
                rows = slice(row, row + own_rows)
                total = (
                    stay_ref[rows, :]
                    + refs[0][rows, :].astype(jnp.float32)
                    + refs[1][rows, :].astype(jnp.float32)
                )
                refs[2][block(own_rows, a * NH + parity), :] = (total * live).astype(
                    jnp.bfloat16
                )

    grad_rows = run(
        add_rows, of((s, width)), (place, counts, stay, from_left, from_right), [SMEM] * 2 + [VMEM] * 3,
        name="add_rows", limit=SMALL,
    )
    quarters1, last = spread(kept1, got1, (grad_rows,))

    def join_out(place_ref, *refs):
        out_ref = refs[-1]
        for i in range(2):
            first = ((place_ref[2] + i) % 2) * n_x
            for k in range(NZ):
                zk = (place_ref[0] + NZ - k) % NZ
                for x in range(n_x):
                    out_ref[:, block(piece, (first + x) * NZ + zk)] = refs[i * NZ + k][
                        :, x * piece : (x + 1) * piece
                    ]

    projected = run(
        join_out, of((own_rows, d)), (place, *quarters0, *quarters1),
        [SMEM] + [VMEM] * (2 * NZ), name="join_out", limit=SMALL,
    )

    def add_terms(a_ref, b_ref, *outs):
        for k in range(NZ):
            cols = slice(k * width, (k + 1) * width)
            outs[k][...] = (
                a_ref[:, cols].astype(jnp.float32) + b_ref[:, cols].astype(jnp.float32)
            ).astype(jnp.bfloat16)

    parts = run(
        add_terms, [of((piece, width))] * NZ, (term_own, term_pair), [VMEM] * 2,
        after=(last, *quarters0[1:]), out_specs=[VMEM] * NZ, name="add_terms", limit=SMALL,
    )
    parts = [parts[0]] + [shift(parts[k], -k) for k in range(1, NZ)]

    def join_term(place_ref, *refs):
        for k in range(NZ):
            refs[-1][block(piece, (place_ref[0] + k) % NZ), :] = refs[k][...].astype(
                jnp.float32
            )

    grad_w = run(
        join_term, of((NZ * piece, width), jnp.float32), (place, *parts),
        [SMEM] + [VMEM] * NZ, after=(projected,), name="join_term", limit=SMALL,
    )
    return (projected[None], grad_rows[None], grad_w)


def solution(mesh):
    placed = (P("dp", None, "tensor"), P("dp", "tensor"), P(), P("dp", "tensor", None))
    return jax.shard_map(
        per_device,
        mesh=mesh,
        in_specs=placed,
        out_specs=(P("dp", "tensor", None), P("dp", None, "tensor"), P("dp", "tensor")),
        check_vma=False,
    )
```

```python
import jax
import jax.numpy as jnp
from jax import lax
from jax.experimental import pallas as pl
from jax.experimental.pallas import tpu as pltpu
from jax.sharding import PartitionSpec as P

HD = 128
NZ = 4
NH = 2
SWAP = [(t, t ^ 1) for t in range(NZ * NH)]
ANY = pl.BlockSpec(memory_space=pl.ANY)
SMEM = pl.BlockSpec(memory_space=pltpu.SMEM)
VMEM = pl.BlockSpec(memory_space=pltpu.VMEM)
BIG = 56 << 20
SMALL = 32 << 20


def ring(step):
    return [
        (z * NH + h, ((z + step) % NZ) * NH + h) for z in range(NZ) for h in range(NH)
    ]


def shift(value, step):
    return lax.ppermute(value, "tensor", ring(step))


def swap(value):
    return lax.ppermute(value, "tensor", SWAP)


def dot(a, b, dims):
    return lax.dot_general(a, b, (dims, ((), ())), preferred_element_type=jnp.float32)


def of(shape, dtype=jnp.bfloat16):
    return jax.ShapeDtypeStruct(shape, dtype)


def run(body, out, args, specs, after=(), grid=(), out_specs=VMEM, name=None, limit=BIG):
    n, m = len(args), len(after)

    def kernel(*refs):
        body(*refs[:n], *refs[n + m :])

    return pl.pallas_call(
        kernel,
        out_shape=out,
        grid=grid,
        in_specs=list(specs) + [ANY] * m,
        out_specs=out_specs,
        name=name,
        cost_estimate=pl.CostEstimate(flops=1000, bytes_accessed=1000, transcendentals=0),
        compiler_params=pltpu.CompilerParams(vmem_limit_bytes=limit),
    )(*args, *after)


def block(rows, start=0):
    return pl.ds(pl.multiple_of(start * rows, rows), rows)


def per_device(attn, w_out, counts, grad_out):
    rank = lax.axis_index("tensor")
    z, h = rank // NH, rank % NH
    s, width = attn.shape[1:]
    own_rows, d = grad_out.shape[1:]
    n_dp = d // w_out.shape[0]
    n_x = n_dp // 2
    piece = w_out.shape[0] // NZ
    feats = n_x * piece
    half = s // 2
    lanes = NZ * width
    y = lax.axis_index("dp") // n_x
    groups = [list(range(n_x)), list(range(n_x, n_dp))]
    pair = [(i, (i + n_x) % n_dp) for i in range(n_dp)]
    place = jnp.stack([z, h, y, rank]).astype(jnp.int32)

    def split_w(place_ref, w_ref, *outs):
        for k in range(NZ):
            outs[k][...] = w_ref[block(piece, (place_ref[0] + k) % NZ), :]

    w_out4 = run(
        split_w, [of((piece, width))] * NZ, (place, w_out), [SMEM, VMEM],
        out_specs=[VMEM] * NZ, name="w_split", limit=SMALL,
    )
    w_near = [w_out4[0]] + [shift(w_out4[k], k) for k in range(1, NZ)]

    def split_g(place_ref, g_ref, *outs):
        for k in range(NZ):
            zk = (place_ref[0] + k) % NZ
            for i in range(2):
                first = ((place_ref[2] + i) % 2) * n_x
                for x in range(n_x):
                    outs[k][:, (i * n_x + x) * piece : (i * n_x + x + 1) * piece] = g_ref[
                        :, block(piece, (first + x) * NZ + zk)
                    ]

    g_out4 = run(
        split_g, [of((own_rows, 2 * feats))] * NZ, (place, grad_out[0]), [SMEM, VMEM],
        after=(w_out4[0],), out_specs=[VMEM] * NZ, name="g_split", limit=SMALL,
    )
    g_near = [g_out4[0]] + [shift(g_out4[k], k) for k in range(1, NZ)]

    def mask_body(place_ref, counts_ref, a_ref, *outs):
        slot = lax.broadcasted_iota(jnp.int32, (1, width), 1) // HD
        live = (slot < counts_ref[place_ref[3]]).astype(jnp.float32).astype(jnp.bfloat16)
        for q in range(2):
            parity = (place_ref[1] + 1 + q) % NH
            for a in range(NZ):
                outs[q][a * own_rows : (a + 1) * own_rows, :] = (
                    a_ref[block(own_rows, a * NH + parity), :] * live
                )

    act = run(
        mask_body, [of((half, width))] * 2, (place, counts, attn[0]), [SMEM, SMEM, VMEM],
        after=(g_out4[0],), out_specs=[VMEM] * 2, name="mask", limit=SMALL,
    )
    left = [shift(act[0], 1), None]
    right = [None, shift(act[1], -1)]
    g_far = [swap(g) for g in g_near]

    def join_w(a, b, c, e, out_ref):
        for k, ref in enumerate((a, b, c, e)):
            out_ref[:, k * width : (k + 1) * width] = ref[...]

    w_own = run(
        join_w, of((piece, lanes)), w_near, [VMEM] * NZ, after=(act[0],), name="w_join", limit=SMALL
    )

    def move(a_ref, out_ref):
        out_ref[...] = a_ref[...]

    w_pair = run(
        move, of((piece, lanes)), (lax.ppermute(w_own, "dp", pair),), [VMEM],
        after=(left[0], right[1], *g_near[1:], g_far[0]), name="w_move",
    )

    def gather(x):
        return lax.all_gather(x, "dp", axis=0, tiled=True, axis_index_groups=groups)

    w_all = [gather(w_own), gather(w_pair)]

    left[1] = shift(act[1], 1)
    right[0] = shift(act[0], -1)
    across = [shift(left[0], 1), shift(right[1], -1)]
    acts = [*act, *left, *across, *right]

    tile = min(256, feats)
    steps = feats // tile

    def project(i, cuts, after):
        part = half // cuts

        def body(w_ref, *refs):
            for q in range(2):
                total = 0.0
                for k in range(NZ):
                    w = w_ref[:, k * width : (k + 1) * width]
                    total += dot(refs[2 * k + q][...], w, ((1,), (1,)))
                if q:
                    refs[8 + cuts][...] = total
                else:
                    for p in range(cuts):
                        refs[8 + p][...] = total[p * part : (p + 1) * part].astype(jnp.bfloat16)

        return run(
            body, [of((part, feats))] * cuts + [of((half, feats), jnp.float32)], (w_all[i], *acts),
            [pl.BlockSpec((tile, lanes), lambda j: (j, 0))] + [VMEM] * 8,
            after=after, grid=(steps,), out_specs=[pl.BlockSpec((r, tile), lambda j: (0, j)) for r in [part] * cuts + [half]],
            name="project", limit=BIG,
        )

    *sent0, kept0 = project(0, 1, ())
    got0 = [swap(x) for x in sent0]

    def join_g(place_ref, *refs):
        for q in range(2):
            for k in range(NZ):
                row = q * NZ + (place_ref[0] + NZ - k) % NZ
                refs[-1][block(own_rows, row), :] = refs[q * NZ + k][...]

    cot = run(
        join_g, of((s, 2 * feats)), (place, *g_far, *g_near), [SMEM] + [VMEM] * (2 * NZ),
        after=(kept0,), name="g_join",
    )

    def term_of(i, after):
        def body(g_ref, *refs):
            top, bottom, out_ref = g_ref[:half, :], g_ref[half:, :], refs[-1]
            for k in range(NZ):
                out_ref[:, k * width : (k + 1) * width] = (
                    dot(top, refs[2 * k][...], ((0,), (0,)))
                    + dot(bottom, refs[2 * k + 1][...], ((0,), (0,)))
                ).astype(jnp.bfloat16)

        return run(
            body, of((feats, lanes)), (cot, *acts),
            [pl.BlockSpec((s, tile), lambda j: (0, i * steps + j))] + [VMEM] * 8,
            after=after, grid=(steps,), out_specs=pl.BlockSpec((tile, lanes), lambda j: (j, 0)),
            name="term", limit=BIG,
        )

    cols = width // 3 if width % 384 == 0 else width

    def rows_term(k, dtypes, after, more=(), q=0):
        def body(g_ref, w_ref, v_ref, *refs):
            total = dot(g_ref[:, :feats], w_ref[...], ((1,), (0,)))
            total += dot(g_ref[:, feats:], v_ref[...], ((1,), (0,)))
            if len(dtypes) == 2:
                refs[0][...] = total[:half].astype(dtypes[0])
                refs[1][...] = total[half:].astype(dtypes[1])
            elif more:
                parts = [total[:half], total[half:]]
                parts[q] += refs[0][...].astype(jnp.float32)
                refs[1][:half, :] = parts[0].astype(dtypes[0])
                refs[1][half:, :] = parts[1].astype(dtypes[0])
            else:
                refs[0][...] = total.astype(dtypes[0])

        n = width // cols
        outs = [of((s // len(dtypes), width), dtype) for dtype in dtypes]
        column = pl.BlockSpec((feats, cols), lambda j: (0, k * n + j))
        return run(
            body, outs, [cot, w_all[0], w_all[1], *more],
            [VMEM, column, column] + [pl.BlockSpec((half, cols), lambda j: (0, j))] * len(more),
            after=after, grid=(n,),
            out_specs=[pl.BlockSpec((o.shape[0], cols), lambda j: (0, j)) for o in outs],
            name="rows_term", limit=BIG,
        )

    def scatter(x):
        return lax.psum_scatter(
            x, "dp", scatter_dimension=0, tiled=True, axis_index_groups=groups
        )

    def settle(place_ref, kept_ref, *refs):
        got, outs = refs[:-NZ], refs[-NZ:]
        near = NZ // len(got)
        for k in range(NZ):
            zk = (place_ref[0] + k) % NZ
            row = block(own_rows, zk % near)
            total = got[0][row, :].astype(jnp.float32)
            if len(got) == 2:
                total = jnp.where(zk < near, total, got[1][row, :].astype(jnp.float32))
            outs[k][...] = (kept_ref[block(own_rows, zk), :] + total).astype(jnp.bfloat16)

    def spread(kept, got, after):
        outs = run(
            settle, [of((own_rows, feats))] * NZ, (place, kept, *got), [SMEM] + [VMEM] * (1 + len(got)),
            after=after, out_specs=[VMEM] * NZ, name="settle",
        )
        return [outs[0]] + [shift(outs[k], k) for k in range(1, NZ)], outs[0]

    bf16, f32 = jnp.bfloat16, jnp.float32
    term_pair = term_of(1, ())
    term_own = term_of(0, (term_pair,))
    far = rows_term(2, (bf16, bf16), (term_own,))
    up = shift(far[0], 1)
    down = shift(far[1], -1)
    *sent1, kept1 = project(1, 1, (far[0],))
    got1 = [swap(x) for x in sent1]
    to_right = rows_term(3, (bf16,), (kept1, *got0), (up,), 0)[0]
    term_pair = run(
        move, of((piece, lanes)), (scatter(term_pair),), [VMEM], after=(to_right,), name="move"
    )
    to_left = rows_term(1, (bf16,), (to_right, term_pair), (down,), 1)[0]
    term_pair = lax.ppermute(term_pair, "dp", pair)
    from_left = shift(to_right, 1)
    from_right = shift(to_left, -1)
    stay = rows_term(0, (f32,), (to_left,))[0]
    quarters0, last = spread(kept0, got0, (stay,))
    term_own = scatter(term_own)

    def add_rows(place_ref, counts_ref, stay_ref, *refs):
        slot = lax.broadcasted_iota(jnp.int32, (1, width), 1) // HD
        live = (slot < counts_ref[place_ref[3]]).astype(jnp.float32)
        for q in range(2):
            parity = (place_ref[1] + 1 + q) % NH
            for a in range(NZ):
                row = q * half + a * own_rows
                rows = slice(row, row + own_rows)
                total = (
                    stay_ref[rows, :]
                    + refs[0][rows, :].astype(jnp.float32)
                    + refs[1][rows, :].astype(jnp.float32)
                )
                refs[2][block(own_rows, a * NH + parity), :] = (total * live).astype(
                    jnp.bfloat16
                )

    grad_rows = run(
        add_rows, of((s, width)), (place, counts, stay, from_left, from_right), [SMEM] * 2 + [VMEM] * 3,
        name="add_rows", limit=SMALL,
    )
    quarters1, last = spread(kept1, got1, (grad_rows,))

    def join_out(place_ref, *refs):
        out_ref = refs[-1]
        for i in range(2):
            first = ((place_ref[2] + i) % 2) * n_x
            for k in range(NZ):
                zk = (place_ref[0] + NZ - k) % NZ
                for x in range(n_x):
                    out_ref[:, block(piece, (first + x) * NZ + zk)] = refs[i * NZ + k][
                        :, x * piece : (x + 1) * piece
                    ]

    projected = run(
        join_out, of((own_rows, d)), (place, *quarters0, *quarters1),
        [SMEM] + [VMEM] * (2 * NZ), name="join_out", limit=SMALL,
    )

    def add_terms(a_ref, b_ref, *outs):
        for k in range(NZ):
            cols = slice(k * width, (k + 1) * width)
            outs[k][...] = (
                a_ref[:, cols].astype(jnp.float32) + b_ref[:, cols].astype(jnp.float32)
            ).astype(jnp.bfloat16)

    parts = run(
        add_terms, [of((piece, width))] * NZ, (term_own, term_pair), [VMEM] * 2,
        after=(last, *quarters0[1:]), out_specs=[VMEM] * NZ, name="add_terms", limit=SMALL,
    )
    parts = [parts[0]] + [shift(parts[k], -k) for k in range(1, NZ)]

    def join_term(place_ref, *refs):
        for k in range(NZ):
            refs[-1][block(piece, (place_ref[0] + k) % NZ), :] = refs[k][...].astype(
                jnp.float32
            )

    grad_w = run(
        join_term, of((NZ * piece, width), jnp.float32), (place, *parts),
        [SMEM] + [VMEM] * NZ, after=(projected,), name="join_term", limit=SMALL,
    )
    return (projected[None], grad_rows[None], grad_w)


def solution(mesh):
    placed = (P("dp", None, "tensor"), P("dp", "tensor"), P(), P("dp", "tensor", None))
    return jax.shard_map(
        per_device,
        mesh=mesh,
        in_specs=placed,
        out_specs=(P("dp", "tensor", None), P("dp", None, "tensor"), P("dp", "tensor")),
        check_vma=False,
    )
```

```python
import jax
import jax.numpy as jnp
from jax import lax
from jax.experimental import pallas as pl
from jax.experimental.pallas import tpu as pltpu
from jax.sharding import PartitionSpec as P

HD = 128
NZ = 4
NH = 2
SWAP = [(t, t ^ 1) for t in range(NZ * NH)]
ANY = pl.BlockSpec(memory_space=pl.ANY)
SMEM = pl.BlockSpec(memory_space=pltpu.SMEM)
VMEM = pl.BlockSpec(memory_space=pltpu.VMEM)
BIG = 56 << 20
SMALL = 32 << 20


def ring(step):
    return [
        (z * NH + h, ((z + step) % NZ) * NH + h) for z in range(NZ) for h in range(NH)
    ]


def shift(value, step):
    return lax.ppermute(value, "tensor", ring(step))


def swap(value):
    return lax.ppermute(value, "tensor", SWAP)


def dot(a, b, dims):
    return lax.dot_general(a, b, (dims, ((), ())), preferred_element_type=jnp.float32)


def of(shape, dtype=jnp.bfloat16):
    return jax.ShapeDtypeStruct(shape, dtype)


def run(body, out, args, specs, after=(), grid=(), out_specs=VMEM, name=None, limit=BIG):
    n, m = len(args), len(after)

    def kernel(*refs):
        body(*refs[:n], *refs[n + m :])

    return pl.pallas_call(
        kernel,
        out_shape=out,
        grid=grid,
        in_specs=list(specs) + [ANY] * m,
        out_specs=out_specs,
        name=name,
        cost_estimate=pl.CostEstimate(flops=1000, bytes_accessed=1000, transcendentals=0),
        compiler_params=pltpu.CompilerParams(vmem_limit_bytes=limit),
    )(*args, *after)


def block(rows, start=0):
    return pl.ds(pl.multiple_of(start * rows, rows), rows)


def per_device(attn, w_out, counts, grad_out):
    rank = lax.axis_index("tensor")
    z, h = rank // NH, rank % NH
    s, width = attn.shape[1:]
    own_rows, d = grad_out.shape[1:]
    n_dp = d // w_out.shape[0]
    n_x = n_dp // 2
    piece = w_out.shape[0] // NZ
    feats = n_x * piece
    half = s // 2
    lanes = NZ * width
    y = lax.axis_index("dp") // n_x
    groups = [list(range(n_x)), list(range(n_x, n_dp))]
    pair = [(i, (i + n_x) % n_dp) for i in range(n_dp)]
    place = jnp.stack([z, h, y, rank]).astype(jnp.int32)

    def split_w(place_ref, w_ref, *outs):
        for k in range(NZ):
            outs[k][...] = w_ref[block(piece, (place_ref[0] + k) % NZ), :]

    w_out4 = run(
        split_w, [of((piece, width))] * NZ, (place, w_out), [SMEM, VMEM],
        out_specs=[VMEM] * NZ, name="w_split", limit=SMALL,
    )
    w_near = [w_out4[0]] + [shift(w_out4[k], k) for k in range(1, NZ)]

    def split_g(place_ref, g_ref, *outs):
        for k in range(NZ):
            zk = (place_ref[0] + k) % NZ
            for i in range(2):
                first = ((place_ref[2] + i) % 2) * n_x
                for x in range(n_x):
                    outs[k][:, (i * n_x + x) * piece : (i * n_x + x + 1) * piece] = g_ref[
                        :, block(piece, (first + x) * NZ + zk)
                    ]

    g_out4 = run(
        split_g, [of((own_rows, 2 * feats))] * NZ, (place, grad_out[0]), [SMEM, VMEM],
        after=(w_out4[0],), out_specs=[VMEM] * NZ, name="g_split", limit=SMALL,
    )
    g_near = [g_out4[0]] + [shift(g_out4[k], k) for k in range(1, NZ)]

    def mask_body(place_ref, counts_ref, a_ref, *outs):
        slot = lax.broadcasted_iota(jnp.int32, (1, width), 1) // HD
        live = (slot < counts_ref[place_ref[3]]).astype(jnp.float32).astype(jnp.bfloat16)
        for q in range(2):
            parity = (place_ref[1] + 1 + q) % NH
            for a in range(NZ):
                outs[q][a * own_rows : (a + 1) * own_rows, :] = (
                    a_ref[block(own_rows, a * NH + parity), :] * live
                )

    act = run(
        mask_body, [of((half, width))] * 2, (place, counts, attn[0]), [SMEM, SMEM, VMEM],
        after=(g_out4[0],), out_specs=[VMEM] * 2, name="mask", limit=SMALL,
    )
    left = [shift(act[0], 1), None]
    right = [None, shift(act[1], -1)]
    g_far = [swap(g) for g in g_near]

    def join_w(a, b, c, e, out_ref):
        for k, ref in enumerate((a, b, c, e)):
            out_ref[:, k * width : (k + 1) * width] = ref[...]

    w_own = run(
        join_w, of((piece, lanes)), w_near, [VMEM] * NZ, after=(act[0],), name="w_join", limit=SMALL
    )

    def move(a_ref, out_ref):
        out_ref[...] = a_ref[...]

    w_pair = run(
        move, of((piece, lanes)), (lax.ppermute(w_own, "dp", pair),), [VMEM],
        after=(left[0], right[1], *g_near[1:], g_far[0]), name="w_move",
    )

    def gather(x):
        return lax.all_gather(x, "dp", axis=0, tiled=True, axis_index_groups=groups)

    w_all = [gather(w_own), gather(w_pair)]

    left[1] = shift(act[1], 1)
    right[0] = shift(act[0], -1)
    across = [shift(left[0], 1), shift(right[1], -1)]
    acts = [*act, *left, *across, *right]

    def join_g(place_ref, *refs):
        for q in range(2):
            for k in range(NZ):
                row = q * NZ + (place_ref[0] + NZ - k) % NZ
                refs[-1][block(own_rows, row), :] = refs[q * NZ + k][...]

    cot = run(
        join_g, of((s, 2 * feats)), (place, *g_far, *g_near), [SMEM] + [VMEM] * (2 * NZ),
        name="g_join",
    )

    tile = min(256, feats)
    steps = feats // tile

    def term_of(i, after):
        def body(g_ref, *refs):
            top, bottom, out_ref = g_ref[:half, :], g_ref[half:, :], refs[-1]
            for k in range(NZ):
                out_ref[:, k * width : (k + 1) * width] = (
                    dot(top, refs[2 * k][...], ((0,), (0,)))
                    + dot(bottom, refs[2 * k + 1][...], ((0,), (0,)))
                ).astype(jnp.bfloat16)

        return run(
            body, of((feats, lanes)), (cot, *acts),
            [pl.BlockSpec((s, tile), lambda j: (0, i * steps + j))] + [VMEM] * 8,
            after=after, grid=(steps,), out_specs=pl.BlockSpec((tile, lanes), lambda j: (j, 0)),
            name="term", limit=BIG,
        )

    def project(i, cuts, after):
        part = half // cuts

        def body(w_ref, *refs):
            for q in range(2):
                total = 0.0
                for k in range(NZ):
                    w = w_ref[:, k * width : (k + 1) * width]
                    total += dot(refs[2 * k + q][...], w, ((1,), (1,)))
                if q:
                    refs[8 + cuts][...] = total
                else:
                    for p in range(cuts):
                        refs[8 + p][...] = total[p * part : (p + 1) * part].astype(jnp.bfloat16)

        return run(
            body, [of((part, feats))] * cuts + [of((half, feats), jnp.float32)], (w_all[i], *acts),
            [pl.BlockSpec((tile, lanes), lambda j: (j, 0))] + [VMEM] * 8,
            after=after, grid=(steps,), out_specs=[pl.BlockSpec((r, tile), lambda j: (0, j)) for r in [part] * cuts + [half]],
            name="project", limit=BIG,
        )

    cols = width // 3 if width % 384 == 0 else width

    def rows_term(k, dtypes, after, more=(), q=0):
        def body(g_ref, w_ref, v_ref, *refs):
            total = dot(g_ref[:, :feats], w_ref[...], ((1,), (0,)))
            total += dot(g_ref[:, feats:], v_ref[...], ((1,), (0,)))
            if len(dtypes) == 2:
                refs[0][...] = total[:half].astype(dtypes[0])
                refs[1][...] = total[half:].astype(dtypes[1])
            elif more:
                parts = [total[:half], total[half:]]
                parts[q] += refs[0][...].astype(jnp.float32)
                refs[1][:half, :] = parts[0].astype(dtypes[0])
                refs[1][half:, :] = parts[1].astype(dtypes[0])
            else:
                refs[0][...] = total.astype(dtypes[0])

        n = width // cols
        outs = [of((s // len(dtypes), width), dtype) for dtype in dtypes]
        column = pl.BlockSpec((feats, cols), lambda j: (0, k * n + j))
        return run(
            body, outs, [cot, w_all[0], w_all[1], *more],
            [VMEM, column, column] + [pl.BlockSpec((half, cols), lambda j: (0, j))] * len(more),
            after=after, grid=(n,),
            out_specs=[pl.BlockSpec((o.shape[0], cols), lambda j: (0, j)) for o in outs],
            name="rows_term", limit=BIG,
        )

    def scatter(x):
        return lax.psum_scatter(
            x, "dp", scatter_dimension=0, tiled=True, axis_index_groups=groups
        )

    def settle(place_ref, kept_ref, *refs):
        got, outs = refs[:-NZ], refs[-NZ:]
        near = NZ // len(got)
        for k in range(NZ):
            zk = (place_ref[0] + k) % NZ
            row = block(own_rows, zk % near)
            total = got[0][row, :].astype(jnp.float32)
            if len(got) == 2:
                total = jnp.where(zk < near, total, got[1][row, :].astype(jnp.float32))
            outs[k][...] = (kept_ref[block(own_rows, zk), :] + total).astype(jnp.bfloat16)

    def spread(kept, got, after):
        outs = run(
            settle, [of((own_rows, feats))] * NZ, (place, kept, *got), [SMEM] + [VMEM] * (1 + len(got)),
            after=after, out_specs=[VMEM] * NZ, name="settle",
        )
        return [outs[0]] + [shift(outs[k], k) for k in range(1, NZ)], outs[0]

    bf16, f32 = jnp.bfloat16, jnp.float32
    term_pair = term_of(1, ())
    far = rows_term(2, (bf16, bf16), (term_pair,))
    up = shift(far[0], 1)
    down = shift(far[1], -1)
    *sent0, kept0 = project(0, 1, (far[0],))
    got0 = [swap(x) for x in sent0]
    stay = rows_term(0, (f32,), (kept0,))[0]
    term_own = term_of(0, (stay, up, down))
    to_right = rows_term(3, (bf16,), (term_own,), (up,), 0)[0]
    term_pair = run(
        move, of((piece, lanes)), (scatter(term_pair),), [VMEM], after=(to_right,), name="move"
    )
    to_left = rows_term(1, (bf16,), (to_right, term_pair), (down,), 1)[0]
    term_pair = lax.ppermute(term_pair, "dp", pair)
    from_left = shift(to_right, 1)
    from_right = shift(to_left, -1)
    *sent1, kept1 = project(1, 1, (to_left, *got0))
    got1 = [swap(x) for x in sent1]
    quarters0, last = spread(kept0, got0, (kept1,))
    term_own = scatter(term_own)

    def add_rows(place_ref, counts_ref, stay_ref, *refs):
        slot = lax.broadcasted_iota(jnp.int32, (1, width), 1) // HD
        live = (slot < counts_ref[place_ref[3]]).astype(jnp.float32)
        for q in range(2):
            parity = (place_ref[1] + 1 + q) % NH
            for a in range(NZ):
                row = q * half + a * own_rows
                rows = slice(row, row + own_rows)
                total = (
                    stay_ref[rows, :]
                    + refs[0][rows, :].astype(jnp.float32)
                    + refs[1][rows, :].astype(jnp.float32)
                )
                refs[2][block(own_rows, a * NH + parity), :] = (total * live).astype(
                    jnp.bfloat16
                )

    grad_rows = run(
        add_rows, of((s, width)), (place, counts, stay, from_left, from_right), [SMEM] * 2 + [VMEM] * 3,
        name="add_rows", limit=SMALL,
    )
    quarters1, last = spread(kept1, got1, (grad_rows,))

    def join_out(place_ref, *refs):
        out_ref = refs[-1]
        for i in range(2):
            first = ((place_ref[2] + i) % 2) * n_x
            for k in range(NZ):
                zk = (place_ref[0] + NZ - k) % NZ
                for x in range(n_x):
                    out_ref[:, block(piece, (first + x) * NZ + zk)] = refs[i * NZ + k][
                        :, x * piece : (x + 1) * piece
                    ]

    projected = run(
        join_out, of((own_rows, d)), (place, *quarters0, *quarters1),
        [SMEM] + [VMEM] * (2 * NZ), name="join_out", limit=SMALL,
    )

    def add_terms(a_ref, b_ref, *outs):
        for k in range(NZ):
            cols = slice(k * width, (k + 1) * width)
            outs[k][...] = (
                a_ref[:, cols].astype(jnp.float32) + b_ref[:, cols].astype(jnp.float32)
            ).astype(jnp.bfloat16)

    parts = run(
        add_terms, [of((piece, width))] * NZ, (term_own, term_pair), [VMEM] * 2,
        after=(last, *quarters0[1:]), out_specs=[VMEM] * NZ, name="add_terms", limit=SMALL,
    )
    parts = [parts[0]] + [shift(parts[k], -k) for k in range(1, NZ)]

    def join_term(place_ref, *refs):
        for k in range(NZ):
            refs[-1][block(piece, (place_ref[0] + k) % NZ), :] = refs[k][...].astype(
                jnp.float32
            )

    grad_w = run(
        join_term, of((NZ * piece, width), jnp.float32), (place, *parts),
        [SMEM] + [VMEM] * NZ, after=(projected,), name="join_term", limit=SMALL,
    )
    return (projected[None], grad_rows[None], grad_w)


def solution(mesh):
    placed = (P("dp", None, "tensor"), P("dp", "tensor"), P(), P("dp", "tensor", None))
    return jax.shard_map(
        per_device,
        mesh=mesh,
        in_specs=placed,
        out_specs=(P("dp", "tensor", None), P("dp", None, "tensor"), P("dp", "tensor")),
        check_vma=False,
    )
```
